128 devices in a mesh: gx: 8 (over x_lo, y), gy: 4 (over x_hi, core), gz: 4 (over z).
Axes of the slice: x: 4 (x_hi: 2, x_lo: 2; x = x_hi * 2 + x_lo), y: 4, z: 4, core: 2. Of those that a mesh axis runs over, the one named last changes fastest.
Arguments:
- hidden_in: bfloat16 [1024, 16384], P(('gy', 'gz'), 'gx'), may hold values from -8 to 8
- norm_gain: bfloat16 [16384], P('gx'), may hold values from 0.099609375 to 1.8984375
- segment_ids: int32 [1024], replicated, may hold values from 0 to 7, never falling along the last dimension, each value on 1 to 256 neighbouring positions
- query_codes: bfloat16 [16384, 16384], P('gx', ('gy', 'gz')), may hold values from -32 to 32
- query_exponents: int32 [128, 256], P('gx', ('gy', 'gz')), may hold values from -1 to 1
- key_codes: bfloat16 [16384, 2, 1024], P('gx', None, ('gy', 'gz')), may hold values from -32 to 32
- key_exponents: int32 [128, 2, 16], P('gx', None, ('gy', 'gz')), may hold values from -1 to 1
- output_codes: bfloat16 [16384, 16384], P(('gy', 'gz'), 'gx'), may hold values from -4 to 4
- output_exponents: int32 [128, 256], P(('gy', 'gz'), 'gx'), may hold values from -1 to 1
Outputs:
- layer_out: bfloat16 [1024, 16384], P(('gy', 'gz'), 'gx')
The draws below stay inside these ranges and needn't reach their ends.
All inputs are finite; a program needn't handle non-finite values.
Results may differ from the reference program's by a relative error of at most 0.038.
Values may be sent and summed in bfloat16 or wider, within the bound.
A program may use at most 64 MiB of HBM per device.

```python
import math
import jax
import jax.numpy as jnp
import numpy as np
from jax import lax

D = 16384
H = 128
KVH = 8
HD = 128
BR = 128
BC = 64
TOKENS = 1024
SEGMENTS = 8
N_GX = 8
N_GY = 4
N_GZ = 4


def draw_hidden_in(key, part):
    key = jax.random.fold_in(key, 11)
    key_rows, key_cols, key_base = jax.random.split(key, 3)
    row_scale = jnp.exp(jax.random.uniform(key_rows, (TOKENS, 1), jnp.float32, 0.0, math.log(10.0)))
    column_place = jnp.arange(D, dtype=jnp.float32)[None, :] / D
    column_scale = jnp.exp(math.log(10.0) * (0.8 * column_place + 0.2 * jax.random.uniform(key_cols, (1, D), jnp.float32)))
    base = jax.random.normal(key_base, (TOKENS, D), jnp.float32)
    base = jnp.clip(base, -4.0, 4.0)
    return (0.02 * base * row_scale * column_scale).astype(jnp.bfloat16)


def draw_query_codes(key, part):
    own = jax.random.fold_in(key, 21)
    noise = jnp.clip(jax.random.normal(own, (D, H * HD), jnp.float32), -4.0, 4.0)
    return noise.astype(jnp.bfloat16)


def draw_key_codes(key, part):
    own = jax.random.fold_in(key, 22)
    noise = jnp.clip(jax.random.normal(own, (D, 2, KVH * HD), jnp.float32), -4.0, 4.0)
    return noise.astype(jnp.bfloat16)


def with_ends(values, key, smallest, top_value):
    index_at = [jax.random.randint(jax.random.fold_in(key, axis), (), 0, length) for axis, length in enumerate(values.shape)]
    widest = values.shape.index(max(values.shape))
    beside = index_at[:widest] + [(index_at[widest] + 1) % values.shape[widest]] + index_at[widest + 1:]
    return values.at[tuple(index_at)].set(smallest).at[tuple(beside)].set(top_value)


def steps_of(stream_key, shape, cuts, smallest, largest):
    gain = 1.0
    for axis_at, blocks in cuts:
        steps = jax.random.uniform(jax.random.fold_in(jax.random.fold_in(stream_key, 6), axis_at), (blocks,), jnp.float32, smallest / len(cuts), largest / len(cuts))
        gain = gain * jnp.repeat(jnp.exp(steps), shape[axis_at] // blocks).reshape((-1,) + (1,) * (len(shape) - 1 - axis_at))
    return gain


def profile(number_of, total, limit, lean):
    loads = [(1 << 20) // math.isqrt(standing ** lean) + 1 for standing in range(2, number_of + 1)]
    rest, counts = total - limit - (number_of - 1), [1] * (number_of - 1)
    while rest > 0:
        candidates = [i for i in range(number_of - 1) if counts[i] < limit]
        pool, remaining = sum([loads[i] for i in candidates]), rest
        for i in candidates:
            extra = min(limit - counts[i], max(1, remaining * loads[i] // pool), rest)
            counts[i] = counts[i] + extra
            rest = rest - extra
    return np.array([limit] + counts)


def uneven_parts(key, amount, total, reach, skew):
    if amount == 2:
        one = jax.random.randint(key, (), max(1, total - reach), min(reach, total - 1) + 1)
        return jnp.stack([one, total - one])
    tallies = jnp.asarray(profile(amount, total, reach, skew), jnp.int32)
    twos = (amount - 1) // 2
    giver, taker = tallies[1:1 + 2 * twos:2], tallies[2:2 + 2 * twos:2]
    slack = jnp.minimum(giver - 1, reach - taker)
    moved = jax.random.randint(jax.random.fold_in(key, 1), (twos,), 0, 1 << 20) % (slack + 1)
    tallies = tallies.at[1:1 + 2 * twos:2].set(giver - moved).at[2:2 + 2 * twos:2].set(taker + moved)
    return tallies[jax.random.permutation(jax.random.fold_in(key, 2), amount)]


def gaussian(own_key, dims, width, bound, shards=(), kind=jnp.bfloat16):
    factor_of = steps_of(own_key, dims, shards, -0.22, 0.18) if shards else 1.0
    array = jax.random.normal(own_key, dims, jnp.float32) * width * factor_of
    return jnp.minimum(jnp.maximum(array, -bound), bound).astype(kind)


def setup_inputs(seed: int = 0) -> dict:
    arg_keys = jax.random.split(jax.random.key(seed), 10)
    return {
        "hidden_in": draw_hidden_in(jax.random.fold_in(arg_keys[9], 71), 0),
        "norm_gain": jnp.clip(1.0 + 0.18 * jax.random.normal(arg_keys[1], (D,), jnp.float32), 0.099609375, 1.8984375).astype(jnp.bfloat16),
        "segment_ids": jnp.searchsorted(jnp.cumsum(uneven_parts(arg_keys[2], SEGMENTS, TOKENS, 2 * TOKENS // SEGMENTS, 2)), jnp.arange(TOKENS), side="right").astype(jnp.int32),
        "query_codes": draw_query_codes(jax.random.fold_in(arg_keys[9], 71), 0),
        "query_exponents": with_ends(jax.random.randint(arg_keys[4], (D // BR, H * HD // BC), -1, 2), jax.random.fold_in(arg_keys[4], 1), -1, 1).astype(jnp.int32),
        "key_codes": draw_key_codes(jax.random.fold_in(arg_keys[9], 71), 0),
        "key_exponents": with_ends(jax.random.randint(arg_keys[6], (D // BR, 2, KVH * HD // BC), -1, 2), jax.random.fold_in(arg_keys[6], 1), -1, 1).astype(jnp.int32),
        "output_codes": gaussian(arg_keys[7], (H * HD, D), 1.0, 4.0, ((0, 16), (1, 8))),
        "output_exponents": with_ends(jax.random.randint(arg_keys[8], (H * HD // BR, D // BC), -1, 2), jax.random.fold_in(arg_keys[8], 1), -1, 1).astype(jnp.int32),
    }


THETA = 500000.0
EPS = 1e-05

def dequant_matrix(codes, exponents, fan_in):
    rows_all, cols_all = codes.shape
    row_blocks, col_blocks = exponents.shape
    scaled = codes.astype(jnp.float32).reshape(row_blocks, rows_all // row_blocks, col_blocks, cols_all // col_blocks)
    scaled = scaled * jnp.exp2(exponents.astype(jnp.float32))[:, None, :, None]
    return (scaled.reshape(rows_all, cols_all) * (1.0 / math.sqrt(fan_in))).astype(jnp.bfloat16)

def dequant_pairs(codes, exponents, fan_in):
    rows_all, pairs, cols_all = codes.shape
    row_blocks, pairs_too, col_blocks = exponents.shape
    scaled = codes.astype(jnp.float32).reshape(row_blocks, rows_all // row_blocks, pairs, col_blocks, cols_all // col_blocks)
    scaled = scaled * jnp.exp2(exponents.astype(jnp.float32))[:, None, :, :, None]
    return (scaled.reshape(rows_all, pairs, cols_all) * (1.0 / math.sqrt(fan_in))).astype(jnp.bfloat16)

def doc_positions(segments):
    count_all = segments.shape[0]
    token_index = jnp.arange(count_all, dtype=jnp.int32)
    begins = jnp.concatenate([jnp.ones((1,), dtype=bool), segments[1:] != segments[:-1]])
    first_index = lax.cummax(jnp.where(begins, token_index, jnp.zeros_like(token_index)), axis=0)
    return (token_index - first_index).astype(jnp.int32)

def rope_tables(positions, half_size):
    exponent = jnp.arange(half_size, dtype=jnp.float32) * (-2.0 * math.log(THETA) / HD)
    frequency = jnp.exp(exponent)
    angles = positions.astype(jnp.float32)[:, None] * frequency[None, :]
    return (jnp.cos(angles), jnp.sin(angles))

def rotate(field, cosine, sine):
    half_size = field.shape[-1] // 2
    first_half = field[..., :half_size]
    second_half = field[..., half_size:]
    return jnp.concatenate([first_half * cosine - second_half * sine, second_half * cosine + first_half * sine], axis=-1)

def attend(queries, query_segments, query_index, keys, values, key_segments, key_index):
    scores = jnp.einsum('qhd,kd->hqk', queries.astype(jnp.float32), keys.astype(jnp.float32)) * (1.0 / math.sqrt(HD))
    allowed = (query_segments[:, None] == key_segments[None, :]) & (key_index[None, :] <= query_index[:, None])
    scores = jnp.where(allowed[None, :, :], scores, -jnp.inf)
    highest = lax.optimization_barrier(jnp.max(scores, axis=2, keepdims=True))
    weights = jnp.exp(scores - highest)
    weights = (weights / lax.optimization_barrier(jnp.sum(weights, axis=2, keepdims=True))).astype(jnp.bfloat16)
    return jnp.einsum('hqk,kd->qhd', weights.astype(jnp.float32), values.astype(jnp.float32)).astype(jnp.bfloat16)

def reference(hidden_in, norm_gain, segment_ids, query_codes, query_exponents, key_codes, key_exponents, output_codes, output_exponents):
    widened = hidden_in.astype(jnp.float32)
    squares = lax.optimization_barrier(jnp.sum(widened * widened, axis=1))
    normed = (widened * lax.rsqrt(squares / D + EPS)[:, None] * norm_gain.astype(jnp.float32)[None, :]).astype(jnp.bfloat16)
    block = D // N_GX
    block_scales = block // BR
    query_sum = jnp.zeros((TOKENS, H * HD), jnp.float32)
    key_sum = jnp.zeros((TOKENS, 2 * KVH * HD), jnp.float32)
    for block_index in range(N_GX):
        piece = normed[:, block_index * block:(block_index + 1) * block]
        query_weight = dequant_matrix(query_codes[block_index * block:(block_index + 1) * block], query_exponents[block_index * block_scales:(block_index + 1) * block_scales], D)
        term = jnp.dot(piece, query_weight, preferred_element_type=jnp.float32).astype(jnp.bfloat16)
        query_sum = query_sum + lax.optimization_barrier(term).astype(jnp.float32)
        key_weight = dequant_pairs(key_codes[block_index * block:(block_index + 1) * block], key_exponents[block_index * block_scales:(block_index + 1) * block_scales], D)
        term = jnp.dot(piece, key_weight.reshape(block, 2 * KVH * HD), preferred_element_type=jnp.float32).astype(jnp.bfloat16)
        key_sum = key_sum + lax.optimization_barrier(term).astype(jnp.float32)
    key_value = key_sum.astype(jnp.bfloat16).reshape(TOKENS, 2, KVH * HD)
    positions = doc_positions(segment_ids)
    cosine, sine = rope_tables(positions, HD // 2)
    queries = rotate(query_sum.reshape(TOKENS, H, HD), cosine[:, None, :], sine[:, None, :]).astype(jnp.bfloat16)
    keys = rotate(key_value[:, 0].astype(jnp.float32).reshape(TOKENS, KVH, HD), cosine[:, None, :], sine[:, None, :]).astype(jnp.bfloat16)
    values = key_value[:, 1].reshape(TOKENS, KVH, HD)
    group = H // KVH
    grouped = queries.reshape(TOKENS, KVH, group, HD).transpose(1, 0, 2, 3)
    token_index = jnp.arange(TOKENS, dtype=jnp.int32)

    def one_group(operands):
        group_queries, group_keys, group_values = operands
        return attend(group_queries, segment_ids, token_index, group_keys, group_values, segment_ids, token_index)
    attended = lax.map(one_group, (grouped, keys.transpose(1, 0, 2), values.transpose(1, 0, 2)))
    attended = attended.transpose(1, 0, 2, 3).reshape(TOKENS, H * HD)
    columns = H * HD // (N_GY * N_GZ)
    column_scales = columns // BR
    mixed = jnp.zeros((TOKENS, D), jnp.float32)
    for group_index in range(N_GY * N_GZ):
        output_weight = dequant_matrix(output_codes[group_index * columns:(group_index + 1) * columns], output_exponents[group_index * column_scales:(group_index + 1) * column_scales], H * HD)
        term = jnp.dot(attended[:, group_index * columns:(group_index + 1) * columns], output_weight, preferred_element_type=jnp.float32).astype(jnp.bfloat16)
        mixed = mixed + lax.optimization_barrier(term).astype(jnp.float32)
    return (widened + mixed).astype(jnp.bfloat16)
```

```python
import math

import jax
import jax.numpy as jnp
import numpy as np
from jax import lax
from jax.experimental import pallas as pl
from jax.experimental.pallas import tpu as pltpu
from jax.sharding import PartitionSpec as P

D = 16384
HD = 128
TOKENS = 1024
THETA = 500000.0
EPS = 1e-05
NC = 4
FEAT = 2048
QC = 1024
QW = QC + 128
F32, BF16 = jnp.float32, jnp.bfloat16
MESH = pl.DeviceIdType.MESH

A_TYPES = ["a_x", "a_zp", "a_zm", "a_s", "a_xzp", "a_xzm", "a_xs", "a_rp", "a_rm", "a_sm", "a_sp", "a_s2"]
B_TYPES = ["b_2p", "b_1p", "b_2m", "b_1m", "b_sp", "b_sm", "b_x"]
C_TYPES = ["c_x", "c_yp", "c_ym", "c_xyp", "c_xym", "c_rp", "c_rm"]
D_TYPES = ["d_s", "d_2p", "d_1p", "d_2m", "d_1m", "d_sp", "d_sm", "d_x"]
TYPES = {name: i for i, name in enumerate(A_TYPES + B_TYPES + C_TYPES + D_TYPES)}

FIRST = (
    ("A0", 0), ("A0", 1), ("DQ", 0), ("A1", 0), ("A2", 0), ("A1", 1), ("A0", 2), ("A3", 0), ("A2", 1), ("MM", 0),
    ("A1", 2), ("A0", 3), ("A3", 1), ("A2", 2), ("B2", 0), ("MM", 1), ("A1", 3), ("A3", 2), ("B3", 0), ("B2", 1),
    ("A2", 3), ("MM", 2), ("B4", 0), ("A3", 3), ("B3", 1), ("B2", 2), ("MM", 3), ("SS", 0), ("B4", 1), ("B3", 2),
    ("B2", 3), ("B4", 2), ("DO", 0), ("B3", 3), ("B4", 3),
)
SECOND = (
    ("C0", 0), ("C0", 1), ("C1", 0), ("C2", 0), ("C1", 1), ("C0", 2), ("C3", 0), ("C2", 1), ("MO", 0), ("C1", 2),
    ("C0", 3), ("C3", 1), ("C2", 2), ("D1", 0), ("MO", 1), ("C1", 3), ("C3", 2), ("D2", 0), ("D1", 1), ("C2", 3),
    ("MO", 2), ("D3", 0), ("C3", 3), ("D2", 1), ("D1", 2), ("MO", 3), ("D4", 0), ("D3", 1), ("D2", 2), ("D1", 3),
    ("D4", 1), ("D3", 2), ("D2", 3), ("D4", 2), ("D3", 3), ("D4", 3),
)


def rope_tables():
    frequency = np.exp(np.arange(HD // 2, dtype=np.float64) * (-2.0 * math.log(THETA) / HD))
    angles = np.arange(TOKENS, dtype=np.float64)[:, None] * frequency[None, :]
    cosine, sine = np.cos(angles), np.sin(angles)
    cosine = np.concatenate([cosine, cosine], axis=1).astype(np.float32)
    sine = np.concatenate([-sine, sine], axis=1).astype(np.float32)
    return cosine.reshape(8, 128, HD), sine.reshape(8, 128, HD)


def layer(
    hid, gain, segs, qc, qe, kc, ke, oc, oe, cos_hbm, sin_hbm, out,
    wq, wk, wo, kct, scale_q, scale_o, cos, sin,
    g, x, squares, sums, sums_in,
    qp, b2, bu, b3, bx, b4, qown,
    kv, kb, vb, qr,
    ag, pp, d_in, dt, d2, du, d3, dx, d4, down,
    send_sem, recv_sem, s_send, s_recv, k_send, k_recv, local,
):
    gx, gy, gz = lax.axis_index("gx"), lax.axis_index("gy"), lax.axis_index("gz")
    xlo, y, xhi, core, z = gx // 4, gx % 4, gy // 2, gy % 2, gz
    yp, ym, y2 = (y + 1) % 4, (y + 3) % 4, (y + 2) % 4
    zp, zm, z2 = (z + 1) % 4, (z + 3) % 4, (z + 2) % 4
    oxlo, oxhi, ocore = 1 - xlo, 1 - xhi, 1 - core
    odd = z % 2
    zo = z + 1 - 2 * odd
    dev_s = (gx, xhi * 2 + ocore, gz)
    dev_xhi = (gx, oxhi * 2 + core, gz)
    dev_zp, dev_zm = (gx, gy, zp), (gx, gy, zm)
    dev_xlo = (oxlo * 4 + y, gy, gz)
    dev_yp, dev_ym = (xlo * 4 + yp, gy, gz), (xlo * 4 + ym, gy, gz)
    peers = [(a, b) for a in range(2) for b in range(4) if (a, b) != (0, 0)]
    dev_peers = [(((xlo + a) % 2) * 4 + (y + b) % 4, gy, gz) for a, b in peers]
    dev_kv = [(0, 1, (gx, gy, zo))]
    for d in (1, 2):
        dev_kv += [(d, 0, ((gx + d) % 8, gy, z)), (d, 1, ((gx + d) % 8, gy, zo))]

    copies = {}

    def fetch(name, index, src, dst):
        copies[name] = pltpu.make_async_copy(src, dst, local.at[index])
        copies[name].start()

    for c in range(NC):
        fetch("hid%d" % c, c, hid.at[pl.ds(16 * c, 16), :], g.at[c, xhi, core, z])
    fetch("kc", 4, kc, kct)
    fetch("qc", 5, qc, wq)
    for d in range(3):
        fetch("cos%d" % d, 6 + d, cos_hbm.at[(gx + 8 - d) % 8], cos.at[d])
        fetch("sin%d" % d, 9 + d, sin_hbm.at[(gx + 8 - d) % 8], sin.at[d])
    fetch("oc", 12, oc, wo)

    barrier = pltpu.get_barrier_semaphore()
    greeted = [dev_s, dev_xhi, dev_zp, dev_zm] + dev_peers
    greeted += [((gx + d) % 8, gy, zo) for d in (1, 2, 6, 7)]
    for other in greeted:
        pl.semaphore_signal(barrier, inc=1, device_id=other, device_id_type=MESH)
    pl.semaphore_wait(barrier, len(greeted))

    sent = []

    def send(name, c, src, dst, to):
        copy = pltpu.make_async_remote_copy(
            src_ref=src, dst_ref=dst, send_sem=send_sem.at[TYPES[name], c], recv_sem=recv_sem.at[TYPES[name], c],
            device_id=to, device_id_type=MESH,
        )
        copy.start()
        sent.append(copy)

    def came(name, c, dst):
        pltpu.make_async_remote_copy(
            src_ref=dst, dst_ref=dst, send_sem=send_sem.at[TYPES[name], c], recv_sem=recv_sem.at[TYPES[name], c],
            device_id=dev_s, device_id_type=MESH,
        ).wait_recv()

    def step_a0(c):
        copies["hid%d" % c].wait()
        own = g.at[c, xhi, core, z]
        send("a_x", c, own, own, dev_xhi)
        send("a_zp", c, own, own, dev_zp)
        send("a_zm", c, own, own, dev_zm)
        send("a_s", c, own, own, dev_s)

    def step_a1(c):
        block = g.at[c, oxhi, core, z]
        came("a_x", c, block)
        send("a_xzp", c, block, block, dev_zp)
        send("a_xzm", c, block, block, dev_zm)
        send("a_xs", c, block, block, dev_s)

    def step_a2(c):
        came("a_zp", c, g.at[c, xhi, core, zm])
        came("a_xzp", c, g.at[c, oxhi, core, zm])
        relay = g.at[c, 0, core, zm]
        send("a_rp", c, relay, relay, dev_zp)
        came("a_zm", c, g.at[c, xhi, core, zp])
        came("a_xzm", c, g.at[c, oxhi, core, zp])
        relay = g.at[c, 1, core, zp]
        send("a_rm", c, relay, relay, dev_zm)
        both = g.at[c, :, core, zm]
        send("a_sm", c, both, both, dev_s)
        both = g.at[c, :, core, zp]
        send("a_sp", c, both, both, dev_s)

    def step_a3(c):
        came("a_rp", c, g.at[c, 0, core, z2])
        came("a_rm", c, g.at[c, 1, core, z2])
        both = g.at[c, :, core, z2]
        send("a_s2", c, both, both, dev_s)

    def step_dq(_):
        rows = lax.broadcasted_iota(jnp.int32, (16, QC), 0)
        cols = lax.broadcasted_iota(jnp.int32, (16, QC), 1)
        spread = jnp.where(rows == cols // 64, 1.0, 0.0).astype(BF16)
        powers = jnp.exp2(qe[...].astype(F32)).astype(BF16)
        scale_q[...] = jnp.dot(powers, spread, preferred_element_type=F32) * (1.0 / 128.0)
        copies["kc"].wait()
        lane = lax.broadcasted_iota(jnp.int32, (1, 128), 1)

        def key_block(k, carry):
            at = pl.multiple_of(k * 128, 128)
            e = jnp.where(lane < 64, ke[0, k], ke[1, k]).astype(F32)
            scale = jnp.exp2(e) * (1.0 / 128.0)
            block = kct[:, pl.ds(at, 128)].astype(F32).T
            wk[pl.ds(at, 128), :] = (block * scale).astype(BF16)
            return carry

        lax.fori_loop(0, 16, key_block, 0)
        copies["qc"].wait()

        def query_block(k, carry):
            at = pl.multiple_of(k * 128, 128)
            scale = scale_q[pl.ds(k, 1), :]
            wq[pl.ds(at, 128), :] = (wq[pl.ds(at, 128), :].astype(F32) * scale).astype(BF16)
            return carry

        lax.fori_loop(0, 16, query_block, 0)
        sums[...] = jnp.zeros_like(sums)

    def step_do(_):
        rows = lax.broadcasted_iota(jnp.int32, (32, FEAT), 0)
        cols = lax.broadcasted_iota(jnp.int32, (32, FEAT), 1)
        spread = jnp.where(rows == cols // 64, 1.0, 0.0).astype(BF16)
        powers = jnp.exp2(oe[...].astype(F32)).astype(BF16)
        scale_o[...] = jnp.dot(powers, spread, preferred_element_type=F32) * (1.0 / 128.0)
        copies["oc"].wait()

        def output_block(k, carry):
            at = pl.multiple_of(k * 128, 128)
            scale = scale_o[pl.ds(k, 1), :]
            wo[pl.ds(at, 128), :] = (wo[pl.ds(at, 128), :].astype(F32) * scale).astype(BF16)
            return carry

        lax.fori_loop(0, 8, output_block, 0)

    def step_mm(c):
        came("a_s", c, g.at[c, xhi, ocore, z])
        came("a_xs", c, g.at[c, oxhi, ocore, z])
        came("a_sm", c, g.at[c, :, ocore, zm])
        came("a_sp", c, g.at[c, :, ocore, zp])
        came("a_s2", c, g.at[c, :, ocore, z2])
        weight = gain[...].astype(F32)

        def scaled(p, carry):
            block = g[c, p // 8, (p // 4) % 2, p % 4].astype(F32)
            at = pl.multiple_of(p * 16, 16)
            x[pl.ds(at, 16), :] = (block * weight).astype(BF16)
            total = block[:, :128] * block[:, :128]
            for k in range(1, FEAT // 128):
                piece = block[:, k * 128:(k + 1) * 128]
                total = total + piece * piece
            squares[pl.ds(at, 16), :] = total
            return carry

        lax.fori_loop(0, 16, scaled, 0)
        sums[c:c + 1, :] = jnp.sum(squares[...].T, axis=0, keepdims=True)

        def columns(n, carry):
            at = pl.multiple_of(n * 256, 256)
            part = jnp.dot(x[...], wq[:, pl.ds(at, 256)], preferred_element_type=F32)
            qp[c, :, :, :, pl.ds(at, 256)] = part.astype(BF16).reshape(2, 4, 32, 256)
            return carry

        lax.fori_loop(0, QC // 256, columns, 0)
        part = jnp.dot(x[...], wk[...], preferred_element_type=F32)
        qp[c, :, :, :, QC:] = part.astype(BF16).reshape(2, 4, 32, 128)
        send("b_2p", c, qp.at[c, 0, y2], b2.at[c, 0], dev_yp)
        send("b_2m", c, qp.at[c, 1, y2], b2.at[c, 1], dev_ym)
        send("b_1p", c, qp.at[c, 1, yp], b3.at[c, 1, 0], dev_yp)
        send("b_1m", c, qp.at[c, 0, ym], b3.at[c, 0, 1], dev_ym)

    def step_b2(c):
        came("b_2p", c, b2.at[c, 0])
        bu[c, 0] = qp[c, 0, yp] + b2[c, 0]
        send("b_sp", c, bu.at[c, 0], b3.at[c, 0, 0], dev_yp)
        came("b_2m", c, b2.at[c, 1])
        bu[c, 1] = qp[c, 1, ym] + b2[c, 1]
        send("b_sm", c, bu.at[c, 1], b3.at[c, 1, 1], dev_ym)

    def step_b3(c):
        came("b_1p", c, b3.at[c, 1, 0])
        came("b_1m", c, b3.at[c, 0, 1])
        came("b_sp", c, b3.at[c, 0, 0])
        came("b_sm", c, b3.at[c, 1, 1])
        total = qp[c, oxlo, y].astype(F32) + b3[c, oxlo, 0].astype(F32) + b3[c, oxlo, 1].astype(F32)
        bx[c] = total.astype(BF16)
        send("b_x", c, bx.at[c], b4.at[c], dev_xlo)
        qown[c] = qp[c, xlo, y].astype(F32) + b3[c, xlo, 0].astype(F32) + b3[c, xlo, 1].astype(F32)

    def step_b4(c):
        came("b_x", c, b4.at[c])
        qown[c] = qown[c] + b4[c].astype(F32)

    def step_ss(_):
        for i, to in enumerate(dev_peers):
            copy = pltpu.make_async_remote_copy(
                src_ref=sums, dst_ref=sums_in.at[i], send_sem=s_send.at[i], recv_sem=s_recv.at[i],
                device_id=to, device_id_type=MESH,
            )
            copy.start()
            sent.append(copy)

    def rotated(field, d):
        return field * cos[d] + pltpu.roll(field, 64, 1) * sin[d]

    def attention():
        total = sums[...]
        for i in range(len(peers)):
            pltpu.make_async_remote_copy(
                src_ref=sums, dst_ref=sums_in.at[i], send_sem=s_send.at[i], recv_sem=s_recv.at[i],
                device_id=dev_s, device_id_type=MESH,
            ).wait_recv()
            total = total + sums_in[i]
        inverse = lax.rsqrt(total * (1.0 / D) + EPS)
        lane = lax.broadcasted_iota(jnp.int32, (32, 256), 1)
        row = lax.broadcasted_iota(jnp.int32, (32, 256), 0)
        factors = []
        for c in range(NC):
            spread = jnp.where(lane == row + 32 * gx, inverse[c:c + 1, :], 0.0)
            factors.append(jnp.sum(spread, axis=1, keepdims=True))
        for c in range(NC):
            own = (qown[c, :, QC:] * factors[c]).astype(BF16)
            kv[0, 0, :, c] = own.reshape(2, 16, 128)
        for i, (d, other, to) in enumerate(dev_kv):
            copy = pltpu.make_async_remote_copy(
                src_ref=kv.at[0, 0], dst_ref=kv.at[d, other], send_sem=k_send.at[i], recv_sem=k_recv.at[i],
                device_id=to, device_id_type=MESH,
            )
            copy.start()
            sent.append(copy)
        for d in range(3):
            copies["cos%d" % d].wait()
            copies["sin%d" % d].wait()
        scaled = [qown[c, :, :QC] * factors[c] for c in range(NC)]
        for h in range(8):
            parts = [scaled[c][:, h * 128:(h + 1) * 128].reshape(2, 1, 16, 128) for c in range(NC)]
            head = jnp.concatenate(parts, axis=1).reshape(128, 128)
            qr[h] = rotated(head, 0).astype(BF16)
        for i, (d, other, to) in enumerate(dev_kv):
            pltpu.make_async_remote_copy(
                src_ref=kv.at[0, 0], dst_ref=kv.at[d, other], send_sem=k_send.at[i], recv_sem=k_recv.at[i],
                device_id=dev_s, device_id_type=MESH,
            ).wait_recv()
        low = lax.broadcasted_iota(jnp.int32, (128, 128), 1) < 64
        for d in range(3):
            at = (2 - d) * 128
            first = kv[d, odd].reshape(128, 128).astype(F32)
            second = kv[d, 1 - odd].reshape(128, 128).astype(F32)
            keys = jnp.where(low, first, pltpu.roll(second, 64, 1))
            kb[at:at + 128, :] = rotated(keys, d).astype(BF16)
            vb[at:at + 128, :] = jnp.where(low, pltpu.roll(first, 64, 1), second).astype(BF16)
        key_segments = jnp.concatenate([segs[pl.ds((gx + 8 - d) % 8, 1), :] for d in (2, 1, 0)], axis=1)
        lane = lax.broadcasted_iota(jnp.int32, (128, 128), 1)
        row = lax.broadcasted_iota(jnp.int32, (128, 128), 0)
        mine = segs[pl.ds(gx, 1), :].astype(F32)
        query_segments = jnp.sum(jnp.where(lane == row, mine, 0.0), axis=1, keepdims=True)
        place = lax.broadcasted_iota(jnp.int32, (128, 384), 1)
        row = lax.broadcasted_iota(jnp.int32, (128, 384), 0)
        allowed = (query_segments == key_segments.astype(F32)) & (place <= row + 256) & (place >= 256 - 128 * gx)
        for h in range(8):
            scores = lax.dot_general(qr[h], kb[...], (((1,), (1,)), ((), ())), preferred_element_type=F32)
            scores = jnp.where(allowed, scores * (1.0 / math.sqrt(HD)), -jnp.inf)
            weights = jnp.exp(scores - jnp.max(scores, axis=1, keepdims=True))
            weights = (weights / jnp.sum(weights, axis=1, keepdims=True)).astype(BF16)
            head = jnp.dot(weights, vb[...], preferred_element_type=F32).astype(BF16).reshape(2, 4, 16, 128)
            for c in range(NC):
                ag[c, xlo, y, :, :, h * 128:(h + 1) * 128] = head[:, c]

    def step_c0(c):
        own = ag.at[c, xlo, y]
        send("c_x", c, own, own, dev_xlo)
        send("c_yp", c, own, own, dev_yp)
        send("c_ym", c, own, own, dev_ym)

    def step_c1(c):
        block = ag.at[c, oxlo, y]
        came("c_x", c, block)
        send("c_xyp", c, block, block, dev_yp)
        send("c_xym", c, block, block, dev_ym)

    def step_c2(c):
        came("c_yp", c, ag.at[c, xlo, ym])
        came("c_xyp", c, ag.at[c, oxlo, ym])
        relay = ag.at[c, 0, ym]
        send("c_rp", c, relay, relay, dev_yp)
        came("c_ym", c, ag.at[c, xlo, yp])
        came("c_xym", c, ag.at[c, oxlo, yp])
        relay = ag.at[c, 1, yp]
        send("c_rm", c, relay, relay, dev_ym)

    def step_c3(c):
        came("c_rp", c, ag.at[c, 0, y2])
        came("c_rm", c, ag.at[c, 1, y2])

    def step_mo(c):
        rows = ag[c].reshape(256, QC)

        def columns(n, carry):
            at = pl.multiple_of(n * 256, 256)
            part = jnp.dot(rows, wo[:, pl.ds(at, 256)], preferred_element_type=F32)
            pp[c, :, :, :, :, pl.ds(at, 256)] = part.astype(BF16).reshape(2, 2, 4, 16, 256)
            return carry

        lax.fori_loop(0, FEAT // 256, columns, 0)
        send("d_s", c, pp.at[c, :, ocore], d_in.at[c], dev_s)

    def step_d1(c):
        came("d_s", c, d_in.at[c])

        def add(w):
            for h in range(2):
                dt[c, h, w] = pp[c, h, core, w] + d_in[c, h, w]

        add(z2)
        send("d_2p", c, dt.at[c, 0, z2], d2.at[c, 0], dev_zp)
        send("d_2m", c, dt.at[c, 1, z2], d2.at[c, 1], dev_zm)
        add(zp)
        send("d_1p", c, dt.at[c, 1, zp], d3.at[c, 1, 0], dev_zp)
        add(zm)
        send("d_1m", c, dt.at[c, 0, zm], d3.at[c, 0, 1], dev_zm)
        add(z)

    def step_d2(c):
        came("d_2p", c, d2.at[c, 0])
        du[c, 0] = dt[c, 0, zp] + d2[c, 0]
        send("d_sp", c, du.at[c, 0], d3.at[c, 0, 0], dev_zp)
        came("d_2m", c, d2.at[c, 1])
        du[c, 1] = dt[c, 1, zm] + d2[c, 1]
        send("d_sm", c, du.at[c, 1], d3.at[c, 1, 1], dev_zm)

    def step_d3(c):
        came("d_1p", c, d3.at[c, 1, 0])
        came("d_1m", c, d3.at[c, 0, 1])
        came("d_sp", c, d3.at[c, 0, 0])
        came("d_sm", c, d3.at[c, 1, 1])
        total = dt[c, oxhi, z].astype(F32) + d3[c, oxhi, 0].astype(F32) + d3[c, oxhi, 1].astype(F32)
        dx[c] = total.astype(BF16)
        send("d_x", c, dx.at[c], d4.at[c], dev_xhi)
        total = dt[c, xhi, z].astype(F32) + d3[c, xhi, 0].astype(F32) + d3[c, xhi, 1].astype(F32)
        down[c] = total + g[c, xhi, core, z].astype(F32)

    def step_d4(c):
        came("d_x", c, d4.at[c])
        out[16 * c:16 * c + 16, :] = (down[c] + d4[c].astype(F32)).astype(BF16)

    table = {
        "A0": step_a0, "A1": step_a1, "A2": step_a2, "A3": step_a3, "DQ": step_dq, "DO": step_do, "MM": step_mm,
        "B2": step_b2, "B3": step_b3, "B4": step_b4, "SS": step_ss, "C0": step_c0, "C1": step_c1, "C2": step_c2,
        "C3": step_c3, "MO": step_mo, "D1": step_d1, "D2": step_d2, "D3": step_d3, "D4": step_d4,
    }
    for name, c in FIRST:
        table[name](c)
    attention()
    for name, c in SECOND:
        table[name](c)
    for copy in sent:
        copy.wait_send()


def shards(hid, gain, segs, qc, qe, kc, ke, oc, oe):
    cosine, sine = rope_tables()
    kct = kc.transpose(1, 2, 0).reshape(128, FEAT)
    ket = ke.transpose(1, 2, 0).reshape(2, 16)
    hbm, vmem, smem = (pl.BlockSpec(memory_space=m) for m in (pl.ANY, pltpu.VMEM, pltpu.SMEM))
    types = len(TYPES)
    scratch = [
        ((FEAT, QC), BF16), ((FEAT, 128), BF16), ((QC, FEAT), BF16), ((128, FEAT), BF16),
        ((16, QC), F32), ((8, FEAT), F32), ((3, 128, HD), F32), ((3, 128, HD), F32),
        ((NC, 2, 2, 4, 16, FEAT), BF16), ((256, FEAT), BF16), ((256, 128), F32), ((8, 256), F32), ((7, 8, 256), F32),
        ((NC, 2, 4, 32, QW), BF16), ((NC, 2, 32, QW), BF16), ((NC, 2, 32, QW), BF16),
        ((NC, 2, 2, 32, QW), BF16), ((NC, 32, QW), BF16), ((NC, 32, QW), BF16), ((NC, 32, QW), F32),
        ((3, 2, 2, 4, 16, 128), BF16), ((384, 128), BF16), ((384, 128), BF16), ((8, 128, 128), BF16),
        ((NC, 2, 4, 2, 16, QC), BF16), ((NC, 2, 2, 4, 16, FEAT), BF16), ((NC, 2, 4, 16, FEAT), BF16),
        ((NC, 2, 4, 16, FEAT), BF16), ((NC, 2, 16, FEAT), BF16), ((NC, 2, 16, FEAT), BF16),
        ((NC, 2, 2, 16, FEAT), BF16), ((NC, 16, FEAT), BF16), ((NC, 16, FEAT), BF16), ((NC, 16, FEAT), F32),
    ]
    scratch = [pltpu.VMEM(shape, dtype) for shape, dtype in scratch]
    dma = pltpu.SemaphoreType.DMA
    scratch += [dma((types, NC)), dma((types, NC)), dma((7,)), dma((7,)), dma((5,)), dma((5,)), dma((13,))]
    return pl.pallas_call(
        layer,
        out_shape=jax.ShapeDtypeStruct((64, FEAT), BF16),
        in_specs=[hbm, vmem, vmem, hbm, vmem, hbm, smem, hbm, vmem, hbm, hbm],
        out_specs=vmem,
        scratch_shapes=scratch,
        compiler_params=pltpu.CompilerParams(collective_id=0, has_side_effects=True, vmem_limit_bytes=60 * 1024 * 1024),
        name="layer",
    )(hid, gain.reshape(1, FEAT), segs.reshape(8, 128), qc, qe, kct, ket, oc, oe, jnp.asarray(cosine), jnp.asarray(sine))


def solution(mesh):
    placed = (
        P(("gy", "gz"), "gx"),
        P("gx"),
        P(),
        P("gx", ("gy", "gz")),
        P("gx", ("gy", "gz")),
        P("gx", None, ("gy", "gz")),
        P("gx", None, ("gy", "gz")),
        P(("gy", "gz"), "gx"),
        P(("gy", "gz"), "gx"),
    )
    return jax.shard_map(shards, mesh=mesh, in_specs=placed, out_specs=P(("gy", "gz"), "gx"), check_vma=False)
```

```python
import math

import jax
import jax.numpy as jnp
import numpy as np
from jax import lax
from jax.experimental import pallas as pl
from jax.experimental.pallas import tpu as pltpu
from jax.sharding import PartitionSpec as P

D = 16384
HD = 128
TOKENS = 1024
THETA = 500000.0
EPS = 1e-05
NC = 4
FEAT = 2048
QC = 1024
QH, OH = 512, 1024
F32, BF16 = jnp.float32, jnp.bfloat16
MESH = pl.DeviceIdType.MESH

UNITS = 2
TYPES = ["a_x", "a_zp", "a_zm", "a_s", "a_xzp", "a_xzm", "a_xs", "a_rp", "a_rm", "a_sm", "a_sp", "a_s2"]
TYPES += ["b_2p", "b_2m", "b_x", "b_p", "b_p_cross", "b_m", "b_m_cross"]
TYPES += ["c_x", "c_yp", "c_ym", "c_xyp", "c_xym", "c_rp", "c_rm"]
TYPES += ["d_s", "d_2p", "d_2m", "d_x", "d_p", "d_p_cross", "d_m", "d_m_cross"]
TYPES = {name: i for i, name in enumerate(TYPES)}

ORDER = (
    ("A0", 0), ("A0", 1), ("A1", 0), ("A0", 2), ("A1", 1), ("A2", 0), ("A1", 2), ("DQ", 0), ("A2", 1), ("A0", 3),
    ("A3", 0), ("HG", 0), ("A1", 3), ("MM", 0), ("A3", 1), ("A2", 2), ("MM", 1), ("HG", 1), ("A2", 3), ("B2", 0),
    ("MM", 11), ("A3", 2), ("MM", 10), ("B2", 1), ("HG", 2), ("A3", 3), ("B2", 11), ("MM", 20), ("HG", 3),
    ("KS", 0), ("DO", 0), ("B2", 10), ("MM", 21), ("B4", 0), ("B2", 20), ("KX", 0), ("MM", 31), ("MM", 30),
    ("B4", 10), ("B4", 1), ("B2", 21), ("KY", 0), ("B2", 31), ("AT", 0), ("B4", 11), ("AT", 1), ("B2", 30),
    ("B4", 20), ("C1", 0), ("B4", 21), ("C1", 1), ("AT", 2), ("C2", 0), ("C2", 1), ("B4", 31), ("B4", 30),
    ("C1", 2), ("AT", 3), ("C3", 0), ("MO", 1), ("C3", 1), ("MO", 11), ("D1", 1), ("C2", 2), ("MO", 10), ("C1", 3),
    ("D1", 11), ("MO", 0), ("D2", 1), ("D1", 10), ("C3", 2), ("MO", 20), ("D2", 11), ("C2", 3), ("D1", 0),
    ("MO", 21), ("D4", 1), ("D1", 20), ("D1", 21), ("D2", 10), ("C3", 3), ("D2", 0), ("MO", 31), ("MO", 30),
    ("D1", 31), ("D1", 30), ("D2", 20), ("D2", 21), ("D2", 31), ("D2", 30), ("D4", 0), ("D4", 21), ("D4", 10),
    ("D4", 20), ("D4", 11), ("D4", 31), ("D4", 30),
)


def rope_tables():
    frequency = np.exp(np.arange(HD // 2, dtype=np.float64) * (-2.0 * math.log(THETA) / HD))
    angles = np.arange(TOKENS, dtype=np.float64)[:, None] * frequency[None, :]
    cosine, sine = np.cos(angles), np.sin(angles)
    cosine = np.concatenate([cosine, cosine], axis=1).astype(np.float32)
    sine = np.concatenate([-sine, sine], axis=1).astype(np.float32)
    return cosine.reshape(8, 128, HD), sine.reshape(8, 128, HD)


def layer(
    hid, gain, segs, qc, qe, kc, ke, oc, oe, cos_hbm, sin_hbm, out,
    wq, wk, wo, kct, scale_q, scale_o, cos, sin,
    g, x, squares, sums, sums_in, factors,
    qp, b2, bu, b3, bx, qown,
    kvp, kv_in, kv, kb, vb, qr,
    ag, pp, d_in, dt, d2, du, d3, dx,
    send_sem, recv_sem, s_send, s_recv, p_send, p_recv, k_send, k_recv, local,
):
    gx, gy, gz = lax.axis_index("gx"), lax.axis_index("gy"), lax.axis_index("gz")
    xlo, y, xhi, core, z = gx // 4, gx % 4, gy // 2, gy % 2, gz
    yp, ym, y2 = (y + 1) % 4, (y + 3) % 4, (y + 2) % 4
    zp, zm, z2 = (z + 1) % 4, (z + 3) % 4, (z + 2) % 4
    oxlo, oxhi, ocore = 1 - xlo, 1 - xhi, 1 - core
    odd = z % 2
    zo = z + 1 - 2 * odd
    dev_s = (gx, xhi * 2 + ocore, gz)
    dev_xhi = (gx, oxhi * 2 + core, gz)
    dev_zp, dev_zm = (gx, gy, zp), (gx, gy, zm)
    dev_xlo = (oxlo * 4 + y, gy, gz)
    dev_yp, dev_ym = (xlo * 4 + yp, gy, gz), (xlo * 4 + ym, gy, gz)
    peers = [(a, b) for a in range(2) for b in range(4) if (a, b) != (0, 0)]
    dev_peers = [(((xlo + a) % 2) * 4 + (y + b) % 4, gy, gz) for a, b in peers]
    dev_kv = [(0, 1, (gx, gy, zo))]
    for d in (1, 2):
        dev_kv += [(d, 0, ((gx + d) % 8, gy, z)), (d, 1, ((gx + d) % 8, gy, zo))]

    copies = {}

    def fetch(name, index, src, dst):
        copies[name] = pltpu.make_async_copy(src, dst, local.at[index])
        copies[name].start()

    for c in range(NC):
        fetch("hid%d" % c, c, hid.at[pl.ds(16 * c, 16), :], g.at[c, xhi, core, z])
    fetch("kc", 4, kc, kct)
    fetch("qc", 5, qc, wq)
    for d in range(3):
        fetch("cos%d" % d, 6 + d, cos_hbm.at[(gx + 8 - d) % 8], cos.at[d])
        fetch("sin%d" % d, 9 + d, sin_hbm.at[(gx + 8 - d) % 8], sin.at[d])
    fetch("oc", 12, oc, wo)

    barrier = pltpu.get_barrier_semaphore()
    greeted = [dev_s, dev_xhi, dev_zp, dev_zm, (gx, oxhi * 2 + core, zp), (gx, oxhi * 2 + core, zm)] + dev_peers
    greeted += [((gx + d) % 8, gy, zo) for d in (1, 2, 6, 7)]
    for other in greeted:
        pl.semaphore_signal(barrier, inc=1, device_id=other, device_id_type=MESH)
    pl.semaphore_wait(barrier, len(greeted))

    sent = []

    def send(name, c, src, dst, to, cross=0):
        copy = pltpu.make_async_remote_copy(
            src_ref=src, dst_ref=dst, send_sem=send_sem.at[TYPES[name] + cross, c],
            recv_sem=recv_sem.at[TYPES[name] + cross, c], device_id=to, device_id_type=MESH,
        )
        copy.start()
        sent.append(copy)

    def came(name, c, dst):
        pltpu.make_async_remote_copy(
            src_ref=dst, dst_ref=dst, send_sem=send_sem.at[TYPES[name], c], recv_sem=recv_sem.at[TYPES[name], c],
            device_id=dev_s, device_id_type=MESH,
        ).wait_recv()

    def send_some(src, dst, sends, recvs, i, to):
        copy = pltpu.make_async_remote_copy(
            src_ref=src, dst_ref=dst, send_sem=sends.at[i], recv_sem=recvs.at[i], device_id=to, device_id_type=MESH,
        )
        copy.start()
        sent.append(copy)

    def came_some(dst, sends, recvs, i):
        pltpu.make_async_remote_copy(
            src_ref=dst, dst_ref=dst, send_sem=sends.at[i], recv_sem=recvs.at[i], device_id=dev_s, device_id_type=MESH,
        ).wait_recv()

    def step_a0(c):
        copies["hid%d" % c].wait()
        own = g.at[c, xhi, core, z]
        send("a_x", c, own, own, dev_xhi)
        send("a_zp", c, own, own, dev_zp)
        send("a_zm", c, own, own, dev_zm)
        send("a_s", c, own, own, dev_s)

    def step_a1(c):
        block = g.at[c, oxhi, core, z]
        came("a_x", c, block)
        send("a_xzp", c, block, block, dev_zp)
        send("a_xzm", c, block, block, dev_zm)
        send("a_xs", c, block, block, dev_s)

    def step_a2(c):
        came("a_zp", c, g.at[c, xhi, core, zm])
        came("a_xzp", c, g.at[c, oxhi, core, zm])
        relay = g.at[c, 0, core, zm]
        send("a_rp", c, relay, relay, dev_zp)
        came("a_zm", c, g.at[c, xhi, core, zp])
        came("a_xzm", c, g.at[c, oxhi, core, zp])
        relay = g.at[c, 1, core, zp]
        send("a_rm", c, relay, relay, dev_zm)
        both = g.at[c, :, core, zm]
        send("a_sm", c, both, both, dev_s)
        both = g.at[c, :, core, zp]
        send("a_sp", c, both, both, dev_s)

    def step_a3(c):
        came("a_rp", c, g.at[c, 0, core, z2])
        came("a_rm", c, g.at[c, 1, core, z2])
        both = g.at[c, :, core, z2]
        send("a_s2", c, both, both, dev_s)

    def step_dq(_):
        rows = lax.broadcasted_iota(jnp.int32, (16, QC), 0)
        cols = lax.broadcasted_iota(jnp.int32, (16, QC), 1)
        spread = jnp.where(rows == cols // 64, 1.0, 0.0).astype(BF16)
        powers = jnp.exp2(qe[...].astype(F32)).astype(BF16)
        scale_q[...] = jnp.dot(powers, spread, preferred_element_type=F32) * (1.0 / 128.0)
        copies["kc"].wait()
        lane = lax.broadcasted_iota(jnp.int32, (1, 128), 1)

        def key_block(k, carry):
            at = pl.multiple_of(k * 128, 128)
            e = jnp.where(lane < 64, ke[0, k], ke[1, k]).astype(F32)
            scale = jnp.exp2(e) * (1.0 / 128.0)
            block = kct[:, pl.ds(at, 128)].astype(F32).T
            wk[pl.ds(at, 128), :] = (block * scale).astype(BF16)
            return carry

        lax.fori_loop(0, 16, key_block, 0)
        copies["qc"].wait()

        def query_block(k, carry):
            at = pl.multiple_of(k * 128, 128)
            scale = scale_q[pl.ds(k, 1), :]
            wq[pl.ds(at, 128), :] = (wq[pl.ds(at, 128), :].astype(F32) * scale).astype(BF16)
            return carry

        lax.fori_loop(0, 16, query_block, 0)
        sums[...] = jnp.zeros_like(sums)

    def step_do(_):
        rows = lax.broadcasted_iota(jnp.int32, (32, FEAT), 0)
        cols = lax.broadcasted_iota(jnp.int32, (32, FEAT), 1)
        spread = jnp.where(rows == cols // 64, 1.0, 0.0).astype(BF16)
        powers = jnp.exp2(oe[...].astype(F32)).astype(BF16)
        scale_o[...] = jnp.dot(powers, spread, preferred_element_type=F32) * (1.0 / 128.0)
        copies["oc"].wait()

        def output_block(k, carry):
            at = pl.multiple_of(k * 128, 128)
            scale = scale_o[pl.ds(k, 1), :]
            wo[pl.ds(at, 128), :] = (wo[pl.ds(at, 128), :].astype(F32) * scale).astype(BF16)
            return carry

        lax.fori_loop(0, 8, output_block, 0)

    def step_hg(c):
        came("a_s", c, g.at[c, xhi, ocore, z])
        came("a_xs", c, g.at[c, oxhi, ocore, z])
        came("a_sm", c, g.at[c, :, ocore, zm])
        came("a_sp", c, g.at[c, :, ocore, zp])
        came("a_s2", c, g.at[c, :, ocore, z2])
        weight = gain[...].astype(F32)

        def scaled(p, carry):
            block = g[c, p // 8, (p // 4) % 2, p % 4].astype(F32)
            at = pl.multiple_of(p * 16, 16)
            x[c, pl.ds(at, 16), :] = (block * weight).astype(BF16)
            total = block[:, :128] * block[:, :128]
            for k in range(1, FEAT // 128):
                piece = block[:, k * 128:(k + 1) * 128]
                total = total + piece * piece
            squares[pl.ds(at, 16), :] = total
            return carry

        lax.fori_loop(0, 16, scaled, 0)
        sums[c:c + 1, :] = jnp.sum(squares[...].T, axis=0, keepdims=True)
        part = jnp.dot(x[c], wk[...], preferred_element_type=F32)
        kvp[:, :, :, c] = part.astype(BF16).reshape(2, 4, 2, 16, 128)

    def step_mm(k):
        c, u = k // 10, k % 10
        i = c * UNITS + u

        def columns(n, carry):
            at = pl.multiple_of(n * 256, 256)
            part = jnp.dot(x[c], wq[:, pl.ds(u * QH + at, 256)], preferred_element_type=F32)
            qp[c, u, :, :, :, pl.ds(at, 256)] = part.astype(BF16).reshape(2, 4, 32, 256)
            return carry

        lax.fori_loop(0, QH // 256, columns, 0)
        send("b_2p", i, qp.at[c, u, 0, y2], b2.at[c, u, 0], dev_yp)
        send("b_2m", i, qp.at[c, u, 1, y2], b2.at[c, u, 1], dev_ym)
        cross = (xlo + 1) % 2
        send("b_p", i, qp.at[c, u, 1, yp], b3.at[c, u, 0, cross], (4 + yp, gy, gz), cross)
        send("b_m", i, qp.at[c, u, 0, ym], b3.at[c, u, 1, xlo], (ym, gy, gz), xlo)
        send("b_x", i, qp.at[c, u, oxlo, y], bx.at[c, u], dev_xlo)

    def step_b2(k):
        c, u = k // 10, k % 10
        i = c * UNITS + u
        came("b_2p", i, b2.at[c, u, 0])
        bu[c, u, 0] = qp[c, u, 0, yp] + b2[c, u, 0]
        send("b_p", i, bu.at[c, u, 0], b3.at[c, u, 0, xlo], (yp, gy, gz), xlo)
        came("b_2m", i, b2.at[c, u, 1])
        bu[c, u, 1] = qp[c, u, 1, ym] + b2[c, u, 1]
        cross = (xlo + 1) % 2
        send("b_m", i, bu.at[c, u, 1], b3.at[c, u, 1, cross], (4 + ym, gy, gz), cross)

    def step_b4(k):
        c, u = k // 10, k % 10
        i = c * UNITS + u
        came("b_x", i, bx.at[c, u])
        came("b_p", i, b3.at[c, u, 0, 0])
        came("b_p_cross", i, b3.at[c, u, 0, 1])
        came("b_m", i, b3.at[c, u, 1, 0])
        came("b_m_cross", i, b3.at[c, u, 1, 1])
        total = qp[c, u, xlo, y].astype(F32) + bx[c, u].astype(F32)
        for direction in range(2):
            for column in range(2):
                total = total + b3[c, u, direction, column].astype(F32)
        qown[c, :, u * QH:(u + 1) * QH] = total

    def step_ks(_):
        for i, to in enumerate(dev_peers):
            send_some(sums, sums_in.at[i], s_send, s_recv, i, to)
            a, b = peers[i]
            send_some(kvp.at[(xlo + a) % 2, (y + b) % 4], kv_in.at[i], p_send, p_recv, i, to)

    def rows_of(table, c):
        return jnp.concatenate([table[c * 16:c * 16 + 16], table[64 + c * 16:64 + c * 16 + 16]], axis=0)

    def rotated(field, cosine, sine):
        return field * cosine + pltpu.roll(field, 64, 1) * sine

    def step_kx(_):
        total = sums[...]
        for i in range(len(peers)):
            came_some(sums_in.at[i], s_send, s_recv, i)
            total = total + sums_in[i]
        inverse = lax.rsqrt(total * (1.0 / D) + EPS)
        lane = lax.broadcasted_iota(jnp.int32, (32, 256), 1)
        row = lax.broadcasted_iota(jnp.int32, (32, 256), 0)
        for c in range(NC):
            spread = jnp.where(lane == row + 32 * gx, inverse[c:c + 1, :], 0.0)
            factors[c] = jnp.broadcast_to(jnp.sum(spread, axis=1, keepdims=True), (32, 128))
        for i in range(len(peers)):
            came_some(kv_in.at[i], p_send, p_recv, i)
        for c in range(NC):
            part = kvp[xlo, y, :, c].astype(F32)
            for i in range(len(peers)):
                part = part + kv_in[i, :, c].astype(F32)
            kv[0, 0, :, c] = (part.reshape(32, 128) * factors[c]).astype(BF16).reshape(2, 16, 128)
        for i, (d, other, to) in enumerate(dev_kv):
            send_some(kv.at[0, 0], kv.at[d, other], k_send, k_recv, i, to)

    def step_ky(_):
        for d in range(3):
            copies["cos%d" % d].wait()
            copies["sin%d" % d].wait()
        for i, (d, other, to) in enumerate(dev_kv):
            came_some(kv.at[d, other], k_send, k_recv, i)
        low = lax.broadcasted_iota(jnp.int32, (128, 128), 1) < 64
        for d in range(3):
            at = (2 - d) * 128
            first = kv[d, odd].reshape(128, 128).astype(F32)
            second = kv[d, 1 - odd].reshape(128, 128).astype(F32)
            keys = jnp.where(low, first, pltpu.roll(second, 64, 1))
            kb[at:at + 128, :] = rotated(keys, cos[d], sin[d]).astype(BF16)
            vb[at:at + 128, :] = jnp.where(low, pltpu.roll(first, 64, 1), second).astype(BF16)

    def step_at(c):
        cosine, sine = rows_of(cos[0], c), rows_of(sin[0], c)
        factor = factors[c]
        for h in range(8):
            head = qown[c, :, h * 128:(h + 1) * 128] * factor
            qr[h * 32:(h + 1) * 32, :] = rotated(head, cosine, sine).astype(BF16)
        row = lax.broadcasted_iota(jnp.int32, (32, 128), 0)
        lane = lax.broadcasted_iota(jnp.int32, (32, 128), 1)
        mine = segs[pl.ds(gx, 1), :].astype(F32)
        token = (row // 16) * 64 + c * 16 + row % 16
        query_segments = jnp.sum(jnp.where(lane == token, mine, 0.0), axis=1, keepdims=True)
        key_segments = jnp.concatenate([segs[pl.ds((gx + 8 - d) % 8, 1), :] for d in (2, 1, 0)], axis=1).astype(F32)
        row = lax.broadcasted_iota(jnp.int32, (32, 384), 0)
        place = lax.broadcasted_iota(jnp.int32, (32, 384), 1)
        token = (row // 16) * 64 + c * 16 + row % 16
        allowed = (query_segments == key_segments) & (place <= token + 256) & (place >= 256 - 128 * gx)
        masked = jnp.where(allowed, 0.0, -jnp.inf)
        scores = lax.dot_general(qr[...], kb[...], (((1,), (1,)), ((), ())), preferred_element_type=F32)
        scores = (scores * (1.0 / math.sqrt(HD))).reshape(8, 32, 384) + masked[None]
        weights = jnp.exp(scores - jnp.max(scores, axis=2, keepdims=True))
        weights = (weights / jnp.sum(weights, axis=2, keepdims=True)).astype(BF16).reshape(256, 384)
        heads = jnp.dot(weights, vb[...], preferred_element_type=F32).astype(BF16)
        for h in range(8):
            ag[c, xlo, y, :, :, h * 128:(h + 1) * 128] = heads[h * 32:(h + 1) * 32].reshape(2, 16, 128)
        own = ag.at[c, xlo, y]
        send("c_x", c, own, own, dev_xlo)
        send("c_yp", c, own, own, dev_yp)
        send("c_ym", c, own, own, dev_ym)

    def step_c1(c):
        block = ag.at[c, oxlo, y]
        came("c_x", c, block)
        send("c_xyp", c, block, block, dev_yp)
        send("c_xym", c, block, block, dev_ym)

    def step_c2(c):
        came("c_yp", c, ag.at[c, xlo, ym])
        came("c_xyp", c, ag.at[c, oxlo, ym])
        relay = ag.at[c, 0, ym]
        send("c_rp", c, relay, relay, dev_yp)
        came("c_ym", c, ag.at[c, xlo, yp])
        came("c_xym", c, ag.at[c, oxlo, yp])
        relay = ag.at[c, 1, yp]
        send("c_rm", c, relay, relay, dev_ym)

    def step_c3(c):
        came("c_rp", c, ag.at[c, 0, y2])
        came("c_rm", c, ag.at[c, 1, y2])

    def step_mo(k):
        c, u = k // 10, k % 10
        i = c * UNITS + u
        rows = ag[c].reshape(256, QC)

        def columns(n, carry):
            at = pl.multiple_of(n * 256, 256)
            part = jnp.dot(rows, wo[:, pl.ds(u * OH + at, 256)], preferred_element_type=F32)
            pp[c, u, :, :, :, :, pl.ds(at, 256)] = part.astype(BF16).reshape(2, 2, 4, 16, 256)
            return carry

        lax.fori_loop(0, OH // 256, columns, 0)
        send("d_s", i, pp.at[c, u, :, ocore], d_in.at[c, u], dev_s)

    def step_d1(k):
        c, u = k // 10, k % 10
        i = c * UNITS + u
        came("d_s", i, d_in.at[c, u])

        def add(w):
            for h in range(2):
                dt[c, u, h, w] = pp[c, u, h, core, w] + d_in[c, u, h, w]

        cross = (xhi + 1) % 2
        add(z2)
        send("d_2p", i, dt.at[c, u, 0, z2], d2.at[c, u, 0], dev_zp)
        send("d_2m", i, dt.at[c, u, 1, z2], d2.at[c, u, 1], dev_zm)
        add(zp)
        send("d_p", i, dt.at[c, u, 1, zp], d3.at[c, u, 0, cross], (gx, 2 + core, zp), cross)
        add(zm)
        send("d_m", i, dt.at[c, u, 0, zm], d3.at[c, u, 1, xhi], (gx, core, zm), xhi)
        add(z)
        send("d_x", i, dt.at[c, u, oxhi, z], dx.at[c, u], dev_xhi)

    def step_d2(k):
        c, u = k // 10, k % 10
        i = c * UNITS + u
        came("d_2p", i, d2.at[c, u, 0])
        du[c, u, 0] = dt[c, u, 0, zp] + d2[c, u, 0]
        send("d_p", i, du.at[c, u, 0], d3.at[c, u, 0, xhi], (gx, core, zp), xhi)
        came("d_2m", i, d2.at[c, u, 1])
        du[c, u, 1] = dt[c, u, 1, zm] + d2[c, u, 1]
        cross = (xhi + 1) % 2
        send("d_m", i, du.at[c, u, 1], d3.at[c, u, 1, cross], (gx, 2 + core, zm), cross)

    def step_d4(k):
        c, u = k // 10, k % 10
        i = c * UNITS + u
        came("d_x", i, dx.at[c, u])
        came("d_p", i, d3.at[c, u, 0, 0])
        came("d_p_cross", i, d3.at[c, u, 0, 1])
        came("d_m", i, d3.at[c, u, 1, 0])
        came("d_m_cross", i, d3.at[c, u, 1, 1])
        columns = slice(u * OH, (u + 1) * OH)
        total = dt[c, u, xhi, z].astype(F32) + dx[c, u].astype(F32)
        for direction in range(2):
            for column in range(2):
                total = total + d3[c, u, direction, column].astype(F32)
        own = g[c, xhi, core, z, :, columns].astype(F32)
        out[16 * c:16 * c + 16, columns] = (own + total).astype(BF16)

    table = {
        "A0": step_a0, "A1": step_a1, "A2": step_a2, "A3": step_a3, "DQ": step_dq, "DO": step_do, "HG": step_hg,
        "MM": step_mm, "B2": step_b2, "B4": step_b4, "KS": step_ks, "KX": step_kx, "KY": step_ky, "AT": step_at,
        "C1": step_c1, "C2": step_c2, "C3": step_c3, "MO": step_mo, "D1": step_d1, "D2": step_d2, "D4": step_d4,
    }
    for name, c in ORDER:
        table[name](c)
    for copy in sent:
        copy.wait_send()


def shards(hid, gain, segs, qc, qe, kc, ke, oc, oe):
    cosine, sine = rope_tables()
    kct = kc.transpose(1, 2, 0).reshape(128, FEAT)
    ket = ke.transpose(1, 2, 0).reshape(2, 16)
    hbm, vmem, smem = (pl.BlockSpec(memory_space=m) for m in (pl.ANY, pltpu.VMEM, pltpu.SMEM))
    types = len(TYPES)
    scratch = [
        ((FEAT, QC), BF16), ((FEAT, 128), BF16), ((QC, FEAT), BF16), ((128, FEAT), BF16),
        ((16, QC), F32), ((8, FEAT), F32), ((3, 128, HD), F32), ((3, 128, HD), F32),
        ((NC, 2, 2, 4, 16, FEAT), BF16), ((NC, 256, FEAT), BF16), ((256, 128), F32),
        ((8, 256), F32), ((7, 8, 256), F32), ((NC, 32, 128), F32),
        ((NC, UNITS, 2, 4, 32, QH), BF16), ((NC, UNITS, 2, 32, QH), BF16), ((NC, UNITS, 2, 32, QH), BF16),
        ((NC, UNITS, 2, 2, 32, QH), BF16), ((NC, UNITS, 32, QH), BF16), ((NC, 32, QC), F32),
        ((2, 4, 2, 4, 16, 128), BF16), ((7, 2, 4, 16, 128), BF16), ((3, 2, 2, 4, 16, 128), BF16),
        ((384, 128), BF16), ((384, 128), BF16), ((256, 128), BF16),
        ((NC, 2, 4, 2, 16, QC), BF16), ((NC, UNITS, 2, 2, 4, 16, OH), BF16), ((NC, UNITS, 2, 4, 16, OH), BF16),
        ((NC, UNITS, 2, 4, 16, OH), BF16), ((NC, UNITS, 2, 16, OH), BF16), ((NC, UNITS, 2, 16, OH), BF16),
        ((NC, UNITS, 2, 2, 16, OH), BF16), ((NC, UNITS, 16, OH), BF16),
    ]
    scratch = [pltpu.VMEM(shape, dtype) for shape, dtype in scratch]
    dma = pltpu.SemaphoreType.DMA
    scratch += [dma((types, NC * UNITS)), dma((types, NC * UNITS))]
    scratch += [dma((7,)), dma((7,)), dma((7,)), dma((7,)), dma((5,)), dma((5,)), dma((13,))]
    return pl.pallas_call(
        layer,
        out_shape=jax.ShapeDtypeStruct((64, FEAT), BF16),
        in_specs=[hbm, vmem, vmem, hbm, vmem, hbm, smem, hbm, vmem, hbm, hbm],
        out_specs=vmem,
        scratch_shapes=scratch,
        compiler_params=pltpu.CompilerParams(collective_id=0, has_side_effects=True, vmem_limit_bytes=60 * 1024 * 1024),
        name="layer",
    )(hid, gain.reshape(1, FEAT), segs.reshape(8, 128), qc, qe, kct, ket, oc, oe, jnp.asarray(cosine), jnp.asarray(sine))


def solution(mesh):
    placed = (
        P(("gy", "gz"), "gx"),
        P("gx"),
        P(),
        P("gx", ("gy", "gz")),
        P("gx", ("gy", "gz")),
        P("gx", None, ("gy", "gz")),
        P("gx", None, ("gy", "gz")),
        P(("gy", "gz"), "gx"),
        P(("gy", "gz"), "gx"),
    )
    return jax.shard_map(shards, mesh=mesh, in_specs=placed, out_specs=P(("gy", "gz"), "gx"), check_vma=False)
```

```python
import math

import jax
import jax.numpy as jnp
import numpy as np
from jax import lax
from jax.experimental import pallas as pl
from jax.experimental.pallas import tpu as pltpu
from jax.sharding import PartitionSpec as P

D = 16384
HD = 128
TOKENS = 1024
THETA = 500000.0
EPS = 1e-05
NC = 4
FEAT = 2048
QC = 1024
QH, OH = 512, 1024
F32, BF16 = jnp.float32, jnp.bfloat16
MESH = pl.DeviceIdType.MESH

UNITS = 2
RECV = {"a_x": NC, "a_p": NC, "a_m": NC, "a_r": NC, "a_s": NC, "b_2": NC * UNITS, "b_3": NC * UNITS, "sums": 1, "kvp": 1}
RECV.update({"kv": 1, "c_x": NC, "c_p": NC, "c_m": NC, "c_r": NC, "d_s": NC * UNITS, "d_2": NC * UNITS, "d_3": NC * UNITS})
SEND = ["a_x", "a_z", "a_s", "b_2", "b_3", "sums", "kvp", "kv", "c_x", "c_y", "d_s", "d_2", "d_3"]
SEND = {name: i for i, name in enumerate(SEND)}

ORDER = (
    ("A0", 0), ("A0", 1), ("A1", 0), ("A0", 2), ("A1", 1), ("A2", 0), ("A1", 2), ("DQ", 0), ("A2", 1), ("A0", 3),
    ("A3", 0), ("HG", 0), ("A1", 3), ("MM", 0), ("A3", 1), ("A2", 2), ("MM", 1), ("HG", 1), ("A2", 3), ("B2", 0),
    ("MM", 11), ("A3", 2), ("MM", 10), ("B2", 1), ("HG", 2), ("A3", 3), ("B2", 11), ("MM", 20), ("HG", 3),
    ("KS", 0), ("DO", 0), ("B2", 10), ("MM", 21), ("B4", 0), ("B2", 20), ("KX", 0), ("MM", 31), ("MM", 30),
    ("B4", 10), ("B4", 1), ("B2", 21), ("KY", 0), ("B2", 31), ("AT", 0), ("B4", 11), ("AT", 1), ("B2", 30),
    ("B4", 20), ("C1", 0), ("B4", 21), ("C1", 1), ("AT", 2), ("C2", 0), ("C2", 1), ("B4", 31), ("B4", 30),
    ("C1", 2), ("AT", 3), ("C3", 0), ("MO", 1), ("C3", 1), ("MO", 11), ("D1", 1), ("C2", 2), ("MO", 10), ("C1", 3),
    ("D1", 11), ("MO", 0), ("D2", 1), ("D1", 10), ("C3", 2), ("MO", 20), ("D2", 11), ("C2", 3), ("D1", 0),
    ("MO", 21), ("D4", 1), ("D1", 20), ("D1", 21), ("D2", 10), ("C3", 3), ("D2", 0), ("MO", 31), ("MO", 30),
    ("D1", 31), ("D1", 30), ("D2", 20), ("D2", 21), ("D2", 31), ("D2", 30), ("D4", 0), ("D4", 21), ("D4", 10),
    ("D4", 20), ("D4", 11), ("D4", 31), ("D4", 30),
)


def rope_tables():
    frequency = np.exp(np.arange(HD // 2, dtype=np.float64) * (-2.0 * math.log(THETA) / HD))
    angles = np.arange(TOKENS, dtype=np.float64)[:, None] * frequency[None, :]
    cosine, sine = np.cos(angles), np.sin(angles)
    cosine = np.concatenate([cosine, cosine], axis=1).astype(np.float32)
    sine = np.concatenate([-sine, sine], axis=1).astype(np.float32)
    return np.stack([cosine.reshape(8, 128, HD), sine.reshape(8, 128, HD)], axis=1)


def layer(
    hid, gain, segs, qc, qe, kc, ke, oc, oe, rope_hbm, out,
    wq, wk, wo, kct, scale_q, scale_o, rope,
    g, x, squares, sums, sums_in, factors,
    qp, b2, bu, b3, qown,
    kvp, kv_in, kv, kb, vb, qr,
    ag, pp, d_in, dt, d2, du, d3,
    send_sem, recv_sem, local,
):
    gx, gy, gz = lax.axis_index("gx"), lax.axis_index("gy"), lax.axis_index("gz")
    xlo, y, xhi, core, z = gx // 4, gx % 4, gy // 2, gy % 2, gz
    yp, ym, y2 = (y + 1) % 4, (y + 3) % 4, (y + 2) % 4
    zp, zm, z2 = (z + 1) % 4, (z + 3) % 4, (z + 2) % 4
    oxlo, oxhi, ocore = 1 - xlo, 1 - xhi, 1 - core
    odd = z % 2
    zo = z + 1 - 2 * odd
    dev_s = (gx, xhi * 2 + ocore, gz)
    dev_xhi = (gx, oxhi * 2 + core, gz)
    dev_zp, dev_zm = (gx, gy, zp), (gx, gy, zm)
    dev_xlo = (oxlo * 4 + y, gy, gz)
    dev_yp, dev_ym = (xlo * 4 + yp, gy, gz), (xlo * 4 + ym, gy, gz)
    peers = [(a, b) for a in range(2) for b in range(4) if (a, b) != (0, 0)]
    dev_peers = [(((xlo + a) % 2) * 4 + (y + b) % 4, gy, gz) for a, b in peers]
    dev_kv = [(1, (gx, gy, zo))]
    for d in (1, 2):
        dev_kv += [(2 * d, ((gx + d) % 8, gy, z)), (2 * d + 1, ((gx + d) % 8, gy, zo))]

    copies = {}

    def fetch(name, index, src, dst):
        copies[name] = pltpu.make_async_copy(src, dst, local.at[index])
        copies[name].start()

    fetch("hid", 0, hid, g.at[:, xhi, core, z])
    fetch("kc", 1, kc, kct)
    fetch("qc", 2, qc, wq)
    for d in range(3):
        pltpu.make_async_copy(rope_hbm.at[(gx + 8 - d) % 8], rope.at[d], local.at[3]).start()
    fetch("oc", 4, oc, wo)

    barrier = pltpu.get_barrier_semaphore()
    greeted = [dev_s, dev_xhi, dev_zp, dev_zm, (gx, oxhi * 2 + core, zp), (gx, oxhi * 2 + core, zm)] + dev_peers
    greeted += [((gx + d) % 8, gy, zo) for d in (1, 2, 6, 7)]
    for other in greeted:
        pl.semaphore_signal(barrier, inc=1, device_id=other, device_id_type=MESH)
    pl.semaphore_wait(barrier, len(greeted))

    first_sem, total = {}, 0
    for name, count in RECV.items():
        first_sem[name] = total
        total += count

    def send(name, i, src, dst, to, group=None):
        pltpu.make_async_remote_copy(
            src_ref=src, dst_ref=dst, send_sem=send_sem.at[SEND[group or name]], recv_sem=recv_sem.at[first_sem[name] + i],
            device_id=to, device_id_type=MESH,
        ).start()

    def came(name, i, dst):
        pltpu.make_async_remote_copy(
            src_ref=dst, dst_ref=dst, send_sem=send_sem.at[0], recv_sem=recv_sem.at[first_sem[name] + i],
            device_id=dev_s, device_id_type=MESH,
        ).wait_recv()

    def left(group, src):
        pltpu.make_async_remote_copy(
            src_ref=src, dst_ref=src, send_sem=send_sem.at[SEND[group]], recv_sem=recv_sem.at[0],
            device_id=dev_s, device_id_type=MESH,
        ).wait_send()

    def step_a0(c):
        if c == 0:
            copies["hid"].wait()
        own = g.at[c, xhi, core, z]
        send("a_x", c, own, own, dev_xhi)
        send("a_p", c, own, own, dev_zp, "a_z")
        send("a_m", c, own, own, dev_zm, "a_z")
        send("a_s", c, own, own, dev_s)

    def step_a1(c):
        block = g.at[c, oxhi, core, z]
        came("a_x", c, block)
        send("a_p", c, block, block, dev_zp, "a_z")
        send("a_m", c, block, block, dev_zm, "a_z")
        send("a_s", c, block, block, dev_s)

    def step_a2(c):
        both = g.at[c, :, core, zm]
        came("a_p", c, both)
        relay = g.at[c, 0, core, zm]
        send("a_r", c, relay, relay, dev_zp, "a_z")
        send("a_s", c, both, both, dev_s)
        both = g.at[c, :, core, zp]
        came("a_m", c, both)
        relay = g.at[c, 1, core, zp]
        send("a_r", c, relay, relay, dev_zm, "a_z")
        send("a_s", c, both, both, dev_s)

    def step_a3(c):
        both = g.at[c, :, core, z2]
        came("a_r", c, both)
        send("a_s", c, both, both, dev_s)

    def step_dq(_):
        rows = lax.broadcasted_iota(jnp.int32, (16, QC), 0)
        cols = lax.broadcasted_iota(jnp.int32, (16, QC), 1)
        spread = jnp.where(rows == cols // 64, 1.0, 0.0).astype(BF16)
        powers = jnp.exp2(qe[...].astype(F32)).astype(BF16)
        scale_q[...] = jnp.dot(powers, spread, preferred_element_type=F32) * (1.0 / 128.0)
        copies["kc"].wait()
        lane = lax.broadcasted_iota(jnp.int32, (1, 128), 1)

        def key_block(k, carry):
            at = pl.multiple_of(k * 128, 128)
            e = jnp.where(lane < 64, ke[0, k], ke[1, k]).astype(F32)
            scale = jnp.exp2(e) * (1.0 / 128.0)
            block = kct[:, pl.ds(at, 128)].astype(F32).T
            wk[pl.ds(at, 128), :] = (block * scale).astype(BF16)
            return carry

        lax.fori_loop(0, 16, key_block, 0)
        copies["qc"].wait()

        def query_block(k, carry):
            at = pl.multiple_of(k * 128, 128)
            scale = scale_q[pl.ds(k, 1), :]
            wq[pl.ds(at, 128), :] = (wq[pl.ds(at, 128), :].astype(F32) * scale).astype(BF16)
            return carry

        lax.fori_loop(0, 16, query_block, 0)
        sums[...] = jnp.zeros_like(sums)

    def step_do(_):
        rows = lax.broadcasted_iota(jnp.int32, (32, FEAT), 0)
        cols = lax.broadcasted_iota(jnp.int32, (32, FEAT), 1)
        spread = jnp.where(rows == cols // 64, 1.0, 0.0).astype(BF16)
        powers = jnp.exp2(oe[...].astype(F32)).astype(BF16)
        scale_o[...] = jnp.dot(powers, spread, preferred_element_type=F32) * (1.0 / 128.0)
        copies["oc"].wait()

        def output_block(k, carry):
            at = pl.multiple_of(k * 128, 128)
            scale = scale_o[pl.ds(k, 1), :]
            wo[pl.ds(at, 128), :] = (wo[pl.ds(at, 128), :].astype(F32) * scale).astype(BF16)
            return carry

        lax.fori_loop(0, 8, output_block, 0)

    def step_hg(c):
        came("a_s", c, g.at[c, :, ocore])
        weight = jnp.concatenate([gain[k:k + 1, :] for k in range(FEAT // 128)], axis=1).astype(F32)

        def scaled(p, carry):
            block = g[c, p // 8, (p // 4) % 2, p % 4].astype(F32)
            at = pl.multiple_of(p * 16, 16)
            x[c, pl.ds(at, 16), :] = (block * weight).astype(BF16)
            total = block[:, :128] * block[:, :128]
            for k in range(1, FEAT // 128):
                piece = block[:, k * 128:(k + 1) * 128]
                total = total + piece * piece
            squares[pl.ds(at, 16), :] = total
            return carry

        lax.fori_loop(0, 16, scaled, 0)
        sums[c:c + 1, :] = jnp.sum(squares[...].T, axis=0, keepdims=True)
        part = jnp.dot(x[c], wk[...], preferred_element_type=F32)
        kvp[:, :, :, c] = part.astype(BF16).reshape(2, 4, 2, 16, 128)

    def step_mm(k):
        c, u = k // 10, k % 10
        i = c * UNITS + u

        def columns(n, carry):
            at = pl.multiple_of(n * 256, 256)
            part = jnp.dot(x[c], wq[:, pl.ds(u * QH + at, 256)], preferred_element_type=F32)
            qp[c, u, :, :, :, pl.ds(at, 256)] = part.astype(BF16).reshape(2, 4, 32, 256)
            return carry

        lax.fori_loop(0, QH // 256, columns, 0)
        send("b_2", i, qp.at[c, u, 0, y2], b2.at[c, u, 0], dev_yp)
        send("b_2", i, qp.at[c, u, 1, y2], b2.at[c, u, 1], dev_ym)
        send("b_3", i, qp.at[c, u, 1, yp], b3.at[c, u, 2 - xlo], (4 + yp, gy, gz))
        send("b_3", i, qp.at[c, u, 0, ym], b3.at[c, u, 3 + xlo], (ym, gy, gz))
        send("b_3", i, qp.at[c, u, oxlo, y], b3.at[c, u, 0], dev_xlo)

    def step_b2(k):
        c, u = k // 10, k % 10
        i = c * UNITS + u
        came("b_2", i, b2.at[c, u])
        bu[c, u, 0] = qp[c, u, 0, yp] + b2[c, u, 0]
        send("b_3", i, bu.at[c, u, 0], b3.at[c, u, 1 + xlo], (yp, gy, gz))
        bu[c, u, 1] = qp[c, u, 1, ym] + b2[c, u, 1]
        send("b_3", i, bu.at[c, u, 1], b3.at[c, u, 4 - xlo], (4 + ym, gy, gz))

    def step_b4(k):
        c, u = k // 10, k % 10
        came("b_3", c * UNITS + u, b3.at[c, u])
        total = qp[c, u, xlo, y].astype(F32)
        for slot in range(5):
            total = total + b3[c, u, slot].astype(F32)
        qown[c, :, u * QH:(u + 1) * QH] = total

    def step_ks(_):
        for i, to in enumerate(dev_peers):
            a, b = peers[i]
            send("sums", 0, sums, sums_in.at[i], to)
            send("kvp", 0, kvp.at[(xlo + a) % 2, (y + b) % 4], kv_in.at[i], to)

    def rows_of(table, c):
        return jnp.concatenate([table[c * 16:c * 16 + 16], table[64 + c * 16:64 + c * 16 + 16]], axis=0)

    def rotated(field, cosine, sine):
        return field * cosine + pltpu.roll(field, 64, 1) * sine

    def step_kx(_):
        came("sums", 0, sums_in)
        total = sums[...]
        for i in range(len(peers)):
            total = total + sums_in[i]
        inverse = lax.rsqrt(total * (1.0 / D) + EPS)
        lane = lax.broadcasted_iota(jnp.int32, (32, 256), 1)
        row = lax.broadcasted_iota(jnp.int32, (32, 256), 0)
        for c in range(NC):
            spread = jnp.where(lane == row + 32 * gx, inverse[c:c + 1, :], 0.0)
            factors[c] = jnp.broadcast_to(jnp.sum(spread, axis=1, keepdims=True), (32, 128))
        came("kvp", 0, kv_in)
        for c in range(NC):
            part = kvp[xlo, y, :, c].astype(F32)
            for i in range(len(peers)):
                part = part + kv_in[i, :, c].astype(F32)
            kv[0, :, c] = (part.reshape(32, 128) * factors[c]).astype(BF16).reshape(2, 16, 128)
        for place, to in dev_kv:
            send("kv", 0, kv.at[0], kv.at[place], to)

    def step_ky(_):
        pltpu.make_async_copy(rope, rope, local.at[3]).wait()
        came("kv", 0, kv.at[pl.ds(1, 5)])
        low = lax.broadcasted_iota(jnp.int32, (128, 128), 1) < 64
        for d in range(3):
            at = (2 - d) * 128
            first = kv[2 * d + odd].reshape(128, 128).astype(F32)
            second = kv[2 * d + 1 - odd].reshape(128, 128).astype(F32)
            keys = jnp.where(low, first, pltpu.roll(second, 64, 1))
            kb[at:at + 128, :] = rotated(keys, rope[d, 0], rope[d, 1]).astype(BF16)
            vb[at:at + 128, :] = jnp.where(low, pltpu.roll(first, 64, 1), second).astype(BF16)

    def step_at(c):
        cosine, sine = rows_of(rope[0, 0], c), rows_of(rope[0, 1], c)
        factor = factors[c]
        for h in range(8):
            head = qown[c, :, h * 128:(h + 1) * 128] * factor
            qr[h * 32:(h + 1) * 32, :] = rotated(head, cosine, sine).astype(BF16)
        row = lax.broadcasted_iota(jnp.int32, (32, 128), 0)
        lane = lax.broadcasted_iota(jnp.int32, (32, 128), 1)
        mine = segs[pl.ds(gx, 1), :].astype(F32)
        token = (row // 16) * 64 + c * 16 + row % 16
        query_segments = jnp.sum(jnp.where(lane == token, mine, 0.0), axis=1, keepdims=True)
        key_segments = jnp.concatenate([segs[pl.ds((gx + 8 - d) % 8, 1), :] for d in (2, 1, 0)], axis=1).astype(F32)
        row = lax.broadcasted_iota(jnp.int32, (32, 384), 0)
        place = lax.broadcasted_iota(jnp.int32, (32, 384), 1)
        token = (row // 16) * 64 + c * 16 + row % 16
        allowed = (query_segments == key_segments) & (place <= token + 256) & (place >= 256 - 128 * gx)
        masked = jnp.where(allowed, 0.0, -jnp.inf)
        scores = lax.dot_general(qr[...], kb[...], (((1,), (1,)), ((), ())), preferred_element_type=F32)
        scores = (scores * (1.0 / math.sqrt(HD))).reshape(8, 32, 384) + masked[None]
        weights = jnp.exp(scores - jnp.max(scores, axis=2, keepdims=True))
        weights = (weights / jnp.sum(weights, axis=2, keepdims=True)).astype(BF16).reshape(256, 384)
        heads = jnp.dot(weights, vb[...], preferred_element_type=F32).astype(BF16)
        for h in range(8):
            ag[c, xlo, y, :, :, h * 128:(h + 1) * 128] = heads[h * 32:(h + 1) * 32].reshape(2, 16, 128)
        own = ag.at[c, xlo, y]
        send("c_x", c, own, own, dev_xlo)
        send("c_p", c, own, own, dev_yp, "c_y")
        send("c_m", c, own, own, dev_ym, "c_y")

    def step_c1(c):
        block = ag.at[c, oxlo, y]
        came("c_x", c, block)
        send("c_p", c, block, block, dev_yp, "c_y")
        send("c_m", c, block, block, dev_ym, "c_y")

    def step_c2(c):
        came("c_p", c, ag.at[c, :, ym])
        relay = ag.at[c, 0, ym]
        send("c_r", c, relay, relay, dev_yp, "c_y")
        came("c_m", c, ag.at[c, :, yp])
        relay = ag.at[c, 1, yp]
        send("c_r", c, relay, relay, dev_ym, "c_y")

    def step_c3(c):
        came("c_r", c, ag.at[c, :, y2])

    def step_mo(k):
        c, u = k // 10, k % 10
        i = c * UNITS + u
        rows = ag[c].reshape(256, QC)

        def columns(n, carry):
            at = pl.multiple_of(n * 256, 256)
            part = jnp.dot(rows, wo[:, pl.ds(u * OH + at, 256)], preferred_element_type=F32)
            pp[c, u, :, :, :, :, pl.ds(at, 256)] = part.astype(BF16).reshape(2, 2, 4, 16, 256)
            return carry

        lax.fori_loop(0, OH // 256, columns, 0)
        send("d_s", i, pp.at[c, u, :, ocore], d_in.at[c, u], dev_s)

    def step_d1(k):
        c, u = k // 10, k % 10
        i = c * UNITS + u
        came("d_s", i, d_in.at[c, u])

        def add(w):
            for h in range(2):
                dt[c, u, h, w] = pp[c, u, h, core, w] + d_in[c, u, h, w]

        add(z2)
        send("d_2", i, dt.at[c, u, 0, z2], d2.at[c, u, 0], dev_zp)
        send("d_2", i, dt.at[c, u, 1, z2], d2.at[c, u, 1], dev_zm)
        add(zp)
        send("d_3", i, dt.at[c, u, 1, zp], d3.at[c, u, 2 - xhi], (gx, 2 + core, zp))
        add(zm)
        send("d_3", i, dt.at[c, u, 0, zm], d3.at[c, u, 3 + xhi], (gx, core, zm))
        add(z)
        send("d_3", i, dt.at[c, u, oxhi, z], d3.at[c, u, 0], dev_xhi)

    def step_d2(k):
        c, u = k // 10, k % 10
        i = c * UNITS + u
        came("d_2", i, d2.at[c, u])
        du[c, u, 0] = dt[c, u, 0, zp] + d2[c, u, 0]
        send("d_3", i, du.at[c, u, 0], d3.at[c, u, 1 + xhi], (gx, core, zp))
        du[c, u, 1] = dt[c, u, 1, zm] + d2[c, u, 1]
        send("d_3", i, du.at[c, u, 1], d3.at[c, u, 4 - xhi], (gx, 2 + core, zm))

    def step_d4(k):
        c, u = k // 10, k % 10
        came("d_3", c * UNITS + u, d3.at[c, u])
        columns = slice(u * OH, (u + 1) * OH)
        total = g[c, xhi, core, z, :, columns].astype(F32) + dt[c, u, xhi, z].astype(F32)
        for slot in range(5):
            total = total + d3[c, u, slot].astype(F32)
        out[16 * c:16 * c + 16, columns] = total.astype(BF16)

    table = {
        "A0": step_a0, "A1": step_a1, "A2": step_a2, "A3": step_a3, "DQ": step_dq, "DO": step_do, "HG": step_hg,
        "MM": step_mm, "B2": step_b2, "B4": step_b4, "KS": step_ks, "KX": step_kx, "KY": step_ky, "AT": step_at,
        "C1": step_c1, "C2": step_c2, "C3": step_c3, "MO": step_mo, "D1": step_d1, "D2": step_d2, "D4": step_d4,
    }
    for name, c in ORDER:
        table[name](c)
    sources = {
        "a_x": g.at[:, 0, 0, 0], "a_z": g.at[pl.ds(0, 3), 0], "a_s": g.at[:, :, 0], "b_2": b2, "b_3": b3,
        "sums": sums_in, "kvp": kv_in, "kv": kv.at[pl.ds(1, 5)], "c_x": ag.at[:, 0, 0], "c_y": ag.at[pl.ds(0, 3)],
        "d_s": d_in, "d_2": d2, "d_3": d3,
    }
    for group, source in sources.items():
        left(group, source)


def shards(hid, gain, segs, qc, qe, kc, ke, oc, oe):
    rope = jnp.asarray(rope_tables())
    kct = kc.transpose(1, 2, 0).reshape(128, FEAT)
    ket = ke.transpose(1, 2, 0).reshape(2, 16)
    hbm, vmem, smem = (pl.BlockSpec(memory_space=m) for m in (pl.ANY, pltpu.VMEM, pltpu.SMEM))
    scratch = [
        ((FEAT, QC), BF16), ((FEAT, 128), BF16), ((QC, FEAT), BF16), ((128, FEAT), BF16),
        ((16, QC), F32), ((8, FEAT), F32), ((3, 2, 128, HD), F32),
        ((NC, 2, 2, 4, 16, FEAT), BF16), ((NC, 256, FEAT), BF16), ((256, 128), F32),
        ((8, 256), F32), ((7, 8, 256), F32), ((NC, 32, 128), F32),
        ((NC, UNITS, 2, 4, 32, QH), BF16), ((NC, UNITS, 2, 32, QH), BF16), ((NC, UNITS, 2, 32, QH), BF16),
        ((NC, UNITS, 5, 32, QH), BF16), ((NC, 32, QC), F32),
        ((2, 4, 2, 4, 16, 128), BF16), ((7, 2, 4, 16, 128), BF16), ((6, 2, 4, 16, 128), BF16),
        ((384, 128), BF16), ((384, 128), BF16), ((256, 128), BF16),
        ((NC, 2, 4, 2, 16, QC), BF16), ((NC, UNITS, 2, 2, 4, 16, OH), BF16), ((NC, UNITS, 2, 4, 16, OH), BF16),
        ((NC, UNITS, 2, 4, 16, OH), BF16), ((NC, UNITS, 2, 16, OH), BF16), ((NC, UNITS, 2, 16, OH), BF16),
        ((NC, UNITS, 5, 16, OH), BF16),
    ]
    scratch = [pltpu.VMEM(shape, dtype) for shape, dtype in scratch]
    dma = pltpu.SemaphoreType.DMA
    scratch += [dma((len(SEND),)), dma((sum(RECV.values()),)), dma((5,))]
    return pl.pallas_call(
        layer,
        out_shape=jax.ShapeDtypeStruct((64, FEAT), BF16),
        in_specs=[hbm, vmem, vmem, hbm, vmem, hbm, smem, hbm, vmem, hbm],
        out_specs=vmem,
        scratch_shapes=scratch,
        compiler_params=pltpu.CompilerParams(collective_id=0, has_side_effects=True, vmem_limit_bytes=60 * 1024 * 1024),
        name="layer",
    )(hid.reshape(NC, 16, FEAT), gain.reshape(16, 128), segs.reshape(8, 128), qc, qe, kct, ket, oc, oe, rope)


def solution(mesh):
    placed = (
        P(("gy", "gz"), "gx"),
        P("gx"),
        P(),
        P("gx", ("gy", "gz")),
        P("gx", ("gy", "gz")),
        P("gx", None, ("gy", "gz")),
        P("gx", None, ("gy", "gz")),
        P(("gy", "gz"), "gx"),
        P(("gy", "gz"), "gx"),
    )
    return jax.shard_map(shards, mesh=mesh, in_specs=placed, out_specs=P(("gy", "gz"), "gx"), check_vma=False)
```

```python
import math

import jax
import jax.numpy as jnp
import numpy as np
from jax import lax
from jax.experimental import pallas as pl
from jax.experimental.pallas import tpu as pltpu
from jax.sharding import PartitionSpec as P

D = 16384
HD = 128
TOKENS = 1024
THETA = 500000.0
EPS = 1e-05
NC = 4
FEAT = 2048
QC = 1024
QH, OH = 512, 1024
F32, BF16 = jnp.float32, jnp.bfloat16
MESH = pl.DeviceIdType.MESH

UNITS = 2
GATHER_A = "b0b0"
GATHER_C = "bb00"
SPLIT_A = "1111"
SPLIT_C = "1111"
SUM_B = "yyyyxgyy"
SUM_D = "ggyyxyyg"
GATHER_COPIES = ("x", "p", "m", "pc", "mc", "r")


def semaphore_names():
    names = []
    for c in range(NC):
        names += [("a_s", c), ("kvp", c)]
        for letter, modes, split in (("a_", GATHER_A, SPLIT_A), ("c_", GATHER_C, SPLIT_C)):
            for k in range(c * 10, c * 10 + int(split[c])):
                names += [(letter + kind, k) for kind in GATHER_COPIES + (("x2",) if modes[c] == "b" else ())]
        for i in (2 * c, 2 * c + 1):
            names += [("d_s", i)]
            for letter, modes in (("b_", SUM_B), ("d_", SUM_D)):
                names += [(letter + kind, i) for kind in ("2", "3") + (("x",) if modes[i] != "g" else ())]
    return names + [("sums", 0), ("sums", 1), ("kv", 0), ("kv", 1)]


RECV = {name: i for i, name in enumerate(semaphore_names())}
SEND = ["a0", "a1", "a_s", "b0", "b1", "sums", "kvp", "kv", "c0", "c1", "d_s", "d0", "d1"]
SEND = {name: i for i, name in enumerate(SEND)}

ORDER = (
    ("A0", 0), ("A0", 10), ("DQ", 0), ("A0", 20), ("A1", 0), ("A1", 10), ("A0", 30), ("A2", 0), ("A1", 30),
    ("A2", 10), ("A3", 0), ("A1", 20), ("HG", 0), ("MM", 1), ("A3", 10), ("A2", 30), ("A2", 20), ("MM", 0),
    ("HG", 1), ("B2", 1), ("MM", 10), ("A3", 30), ("B2", 0), ("A3", 20), ("MM", 11), ("HG", 2), ("B2", 10),
    ("HG", 3), ("MM", 20), ("B2", 11), ("MM", 31), ("B3", 1), ("KX", 0), ("B3", 10), ("KX", 1), ("B3", 11),
    ("MM", 21), ("B1", 20), ("B3", 0), ("MM", 30), ("B2", 31), ("B4", 1), ("KY", 0), ("B2", 21), ("B4", 10),
    ("B4", 11), ("AT", 1), ("C0", 10), ("B2", 20), ("B4", 0), ("AT", 0), ("B2", 30), ("C0", 0), ("DO", 0),
    ("B3", 31), ("C1", 10), ("B4", 20), ("B4", 21), ("B3", 30), ("AT", 2), ("C0", 20), ("C2", 10), ("C1", 0),
    ("B4", 31), ("B4", 30), ("AT", 3), ("C0", 30), ("C1", 20), ("C2", 0), ("C3", 10), ("MO", 11), ("C1", 30),
    ("MO", 10), ("D0", 11), ("C2", 20), ("C3", 0), ("MO", 1), ("D0", 10), ("MO", 0), ("D0", 1), ("C2", 30),
    ("D2", 11), ("C3", 20), ("D0", 0), ("MO", 20), ("MO", 21), ("D2", 1), ("D2", 10), ("D0", 20), ("C3", 30),
    ("MO", 30), ("D0", 21), ("MO", 31), ("D3", 11), ("D0", 30), ("D3", 10), ("D0", 31), ("D2", 30), ("D2", 21),
    ("D4", 1), ("D1", 20), ("D4", 11), ("D2", 0), ("D2", 31), ("D3", 30), ("D3", 21), ("D2", 20), ("D4", 10),
    ("D4", 30), ("D4", 20), ("D4", 0), ("D4", 21), ("D4", 31),
)


START = [c for name, c in ORDER if name == "A0"][0]


def rope_tables():
    frequency = np.exp(np.arange(HD // 2, dtype=np.float64) * (-2.0 * math.log(THETA) / HD))
    angles = np.arange(TOKENS, dtype=np.float64)[:, None] * frequency[None, :]
    cosine, sine = np.cos(angles), np.sin(angles)
    cosine = np.concatenate([cosine, cosine], axis=1).astype(np.float32)
    sine = np.concatenate([-sine, sine], axis=1).astype(np.float32)
    return np.stack([cosine.reshape(8, 128, HD), sine.reshape(8, 128, HD)], axis=1)


def layer(
    hid, gain_hbm, segs_hbm, qc, qe_hbm, kc, ke_hbm, oc, oe_hbm, rope_hbm, out,
    gain, segs, qe, ke, oe,
    wq, wk, wo, kct, scale_q, scale_o, rope,
    g, x, squares, sums, sums_in, factors,
    qp, b2, bu, b3, bx, qown,
    kvp, kv_in, kv, kb, vb, qr,
    ag, pp, d_in, dt, d2, du, d3, dx,
    send_sem, recv_sem, local,
):
    gx, gy, gz = lax.axis_index("gx"), lax.axis_index("gy"), lax.axis_index("gz")
    xlo, y, xhi, core, z = gx // 4, gx % 4, gy // 2, gy % 2, gz
    yp, ym, y2 = (y + 1) % 4, (y + 3) % 4, (y + 2) % 4
    zp, zm, z2 = (z + 1) % 4, (z + 3) % 4, (z + 2) % 4
    oxlo, oxhi, ocore = 1 - xlo, 1 - xhi, 1 - core
    odd = z % 2
    zo = z + 1 - 2 * odd
    dev_s = (gx, xhi * 2 + ocore, gz)
    dev_xhi = (gx, oxhi * 2 + core, gz)
    dev_zp, dev_zm = (gx, gy, zp), (gx, gy, zm)
    dev_xlo = (oxlo * 4 + y, gy, gz)
    dev_yp, dev_ym = (xlo * 4 + yp, gy, gz), (xlo * 4 + ym, gy, gz)
    peers = [(a, b) for a in range(2) for b in range(4) if (a, b) != (0, 0)]
    dev_peers = [(((xlo + a) % 2) * 4 + (y + b) % 4, gy, gz) for a, b in peers]
    dev_kv = [(1, (gx, gy, zo))]
    for d in (1, 2):
        dev_kv += [(2 * d, ((gx + d) % 8, gy, z)), (2 * d + 1, ((gx + d) % 8, gy, zo))]

    barrier = pltpu.get_barrier_semaphore()
    greeted = [(gx, oxhi * 2 + core, (z + d) % 4) for d in (2, 1, 3, 0)] + [(gx, gy, (z + d) % 4) for d in (2, 1, 3)]
    greeted += [dev_s] + dev_peers
    greeted += [((gx + d) % 8, gy, zo) for d in (1, 2, 6, 7)]
    for other in greeted:
        pl.semaphore_signal(barrier, inc=1, device_id=other, device_id_type=MESH)

    copies = {}

    def fetch(name, index, src, dst):
        copies[name] = pltpu.make_async_copy(src, dst, local.at[index])
        copies[name].start()

    fetch("hid", 0, hid, g.at[:, xhi, core, z])
    fetch("ke", 5, ke_hbm, ke)
    fetch("qe", 6, qe_hbm, qe)
    fetch("kc", 1, kc, kct)
    fetch("qc", 2, qc, wq)
    for d in range(3):
        pltpu.make_async_copy(rope_hbm.at[(gx + 8 - d) % 8], rope.at[d], local.at[3]).start()
    fetch("gain", 7, gain_hbm, gain)
    fetch("segs", 8, segs_hbm, segs)
    fetch("oe", 9, oe_hbm, oe)
    fetch("oc", 4, oc, wo)

    pl.semaphore_wait(barrier, len(greeted))

    def send(name, i, src, dst, to, group):
        pltpu.make_async_remote_copy(
            src_ref=src, dst_ref=dst, send_sem=send_sem.at[SEND[group]], recv_sem=recv_sem.at[RECV[name, i]],
            device_id=to, device_id_type=MESH,
        ).start()

    def came(name, i, dst):
        pltpu.make_async_remote_copy(
            src_ref=dst, dst_ref=dst, send_sem=send_sem.at[0], recv_sem=recv_sem.at[RECV[name, i]],
            device_id=dev_s, device_id_type=MESH,
        ).wait_recv()

    def left(group, src):
        pltpu.make_async_remote_copy(
            src_ref=src, dst_ref=src, send_sem=send_sem.at[SEND[group]], recv_sem=recv_sem.at[0],
            device_id=dev_s, device_id_type=MESH,
        ).wait_send()

    def gather(letter, modes, split, blocks, width, h, w, device, neighbour):
        oh, wp, wm, w2 = 1 - h, (w + 1) % 4, (w + 3) % 4, (w + 2) % 4
        across, plus, minus = device(oh, w), device(h, wp), device(h, wm)

        def mode(k):
            return modes[k // 10]

        def buffer(k, column, at, piece=0, pieces=1):
            count = int(split[k // 10]) * pieces
            return blocks(k // 10, column, at, pl.ds((k % 10 * pieces + piece) * (width // count), width // count))

        def copy(kind, k, block, to):
            send(letter + "_" + kind, k, block, block, to, letter + str(k // 20))

        def await_block(kind, k, block):
            came(letter + "_" + kind, k, block)

        def first(k):
            own = buffer(k, h, w)
            copy("x", k, own, across)
            copy("p", k, own, plus)
            copy("m", k, own, minus)
            neighbour(k, own)
            if mode(k) == "D":
                copy("r", k, own, device(h, w2))
                copy("pc", k, own, device(oh, wp))
                copy("mc", k, own, device(oh, wm))
                copy("r", k, own, device(oh, w2))

        def second(k):
            if mode(k) == "b":
                await_block("p", k, buffer(k, h, wm))
                copy("r", k, buffer(k, h, wm, 0, 2), plus)
                neighbour(k, buffer(k, h, wm))
                await_block("m", k, buffer(k, h, wp))
                copy("r", k, buffer(k, h, wp, 1, 2), minus)
                neighbour(k, buffer(k, h, wp))
            block = buffer(k, oh, w)
            await_block("x", k, block)
            copy("pc", k, block, plus)
            copy("mc", k, block, minus)
            neighbour(k, block)

        def third(k):
            if mode(k) == "b":
                block = buffer(k, h, w2)
                await_block("r", k, block)
                copy("x2", k, block, across)
                neighbour(k, block)
                return
            await_block("p", k, buffer(k, h, wm))
            await_block("pc", k, buffer(k, oh, wm))
            copy("r", k, buffer(k, 0, wm), plus)
            await_block("m", k, buffer(k, h, wp))
            await_block("mc", k, buffer(k, oh, wp))
            copy("r", k, buffer(k, 1, wp), minus)
            neighbour(k, buffer(k, slice(None), wm))
            neighbour(k, buffer(k, slice(None), wp))

        def fourth(k):
            if mode(k) == "b":
                for kind, at in (("pc", wm), ("mc", wp), ("x2", w2)):
                    block = buffer(k, oh, at)
                    await_block(kind, k, block)
                    neighbour(k, block)
                return
            if mode(k) == "D":
                await_block("x", k, buffer(k, oh, w))
                neighbour(k, buffer(k, oh, w))
                for kind, at in (("p", wm), ("m", wp)):
                    await_block(kind, k, buffer(k, h, at))
                    await_block(kind + "c", k, buffer(k, oh, at))
                    neighbour(k, buffer(k, slice(None), at))
            both = buffer(k, slice(None), w2)
            await_block("r", k, both)
            neighbour(k, both)

        return first, second, third, fourth

    def scatter(letter, modes, part, r2, ru, r3, rx, width, h, w, device, finish):
        oh, wp, wm, w2 = 1 - h, (w + 1) % 4, (w + 3) % 4, (w + 2) % 4
        across, plus, minus = device(oh, w), device(h, wp), device(h, wm)
        low, high = pl.ds(0, width // 2), pl.ds(width // 2, width // 2)

        def copy(kind, k, src, dst, to):
            i = k // 10 * UNITS + k % 10
            send(letter + "_" + kind, i, src, dst, to, letter + str(k // 20))

        def await_blocks(kind, k, blocks):
            came(letter + "_" + kind, k // 10 * UNITS + k % 10, blocks)

        def mode(k):
            return modes[k // 10 * UNITS + k % 10]

        def begin(k):
            c, u = k // 10, k % 10
            if mode(k) == "x":
                copy("x", k, part.at[c, u, oh], rx.at[c, u], across)
                return
            copy("2", k, part.at[c, u, 0, w2], r2.at[c, u, 0], plus)
            copy("2", k, part.at[c, u, 1, w2], r2.at[c, u, 1], minus)
            if mode(k) == "g":
                copy("3", k, part.at[c, u, 1, wp], r3.at[c, u, 2 - h], device(1, wp))
                copy("3", k, part.at[c, u, 0, wm], r3.at[c, u, 3 + h], device(0, wm))
                copy("3", k, part.at[c, u, oh, w], r3.at[c, u, 0], across)
            else:
                copy("3", k, part.at[c, u, 1, wp], r3.at[c, u, 2], plus)
                copy("3", k, part.at[c, u, 0, wm], r3.at[c, u, 3], minus)

        def one(k):
            c, u = k // 10, k % 10
            await_blocks("x", k, rx.at[c, u])

            def add(at):
                part[c, u, h, at] = part[c, u, h, at] + rx[c, u, at]

            add(w2)
            copy("2", k, part.at[c, u, h, w2, :, low], r2.at[c, u, 0, :, low], plus)
            copy("2", k, part.at[c, u, h, w2, :, high], r2.at[c, u, 1, :, high], minus)
            add(wp)
            copy("3", k, part.at[c, u, h, wp, :, high], r3.at[c, u, 1, :, high], plus)
            add(wm)
            copy("3", k, part.at[c, u, h, wm, :, low], r3.at[c, u, 3, :, low], minus)
            add(w)

        def two(k):
            c, u = k // 10, k % 10
            if mode(k) == "x":
                await_blocks("2", k, r2.at[c, u, 0])
                ru[c, u, 0, :, low] = part[c, u, h, wp, :, low] + r2[c, u, 0, :, low]
                copy("3", k, ru.at[c, u, 0, :, low], r3.at[c, u, 1, :, low], plus)
                ru[c, u, 1, :, high] = part[c, u, h, wm, :, high] + r2[c, u, 1, :, high]
                copy("3", k, ru.at[c, u, 1, :, high], r3.at[c, u, 3, :, high], minus)
                return
            await_blocks("2", k, r2.at[c, u])
            ru[c, u, 0] = part[c, u, 0, wp] + r2[c, u, 0]
            if mode(k) == "g":
                copy("3", k, ru.at[c, u, 0], r3.at[c, u, 1 + h], device(0, wp))
            else:
                copy("3", k, ru.at[c, u, 0], r3.at[c, u, 1], plus)
            ru[c, u, 1] = part[c, u, 1, wm] + r2[c, u, 1]
            if mode(k) == "g":
                copy("3", k, ru.at[c, u, 1], r3.at[c, u, 4 - h], device(1, wm))
            else:
                copy("3", k, ru.at[c, u, 1], r3.at[c, u, 4], minus)

        def three(k):
            c, u = k // 10, k % 10
            await_blocks("3", k, r3.at[c, u, pl.ds(1, 4)])
            total = part[c, u, oh, w].astype(F32) + r3[c, u, 1 + oh].astype(F32) + r3[c, u, 3 + oh].astype(F32)
            part[c, u, oh, w] = total.astype(BF16)
            copy("x", k, part.at[c, u, oh, w], r3.at[c, u, 0], across)

        def four(k):
            c, u = k // 10, k % 10
            total = part[c, u, h, w].astype(F32)
            if mode(k) == "g":
                await_blocks("3", k, r3.at[c, u])
                slots = range(5)
            elif mode(k) == "y":
                await_blocks("x", k, r3.at[c, u, 0])
                slots = (0, 1 + h, 3 + h)
            else:
                await_blocks("3", k, r3.at[c, u, pl.ds(1, 2)])
                slots = (1, 3)
            for slot in slots:
                total = total + r3[c, u, slot].astype(F32)
            finish(c, u, total)

        return begin, one, two, three, four

    def to_core(k, block):
        send("a_s", k // 10, block, block, dev_s, "a_s")

    gather_a = gather(
        "a", GATHER_A, SPLIT_A, lambda c, h, w, some: g.at[c, h, core, w, :, some], FEAT,
        xhi, z, lambda h, w: (gx, h * 2 + core, w), to_core,
    )

    def step_dq(_):
        rows = lax.broadcasted_iota(jnp.int32, (16, QC), 0)
        cols = lax.broadcasted_iota(jnp.int32, (16, QC), 1)
        spread = jnp.where(rows == cols // 64, 1.0, 0.0).astype(BF16)
        copies["qe"].wait()
        copies["ke"].wait()
        copies["gain"].wait()
        powers = jnp.exp2(qe[...].astype(F32)).astype(BF16)
        scale_q[...] = jnp.dot(powers, spread, preferred_element_type=F32) * (1.0 / 128.0)
        copies["kc"].wait()
        lane = lax.broadcasted_iota(jnp.int32, (1, 128), 1)

        def key_block(k, carry):
            at = pl.multiple_of(k * 128, 128)
            e = jnp.where(lane < 64, ke[0, k], ke[1, k]).astype(F32)
            scale = jnp.exp2(e) * (1.0 / 128.0)
            block = kct[:, pl.ds(at, 128)].astype(F32).T
            wk[pl.ds(at, 128), :] = (block * scale).astype(BF16)
            return carry

        lax.fori_loop(0, 16, key_block, 0)
        copies["qc"].wait()

        def query_block(k, carry):
            at = pl.multiple_of(k * 128, 128)
            scale = scale_q[pl.ds(k, 1), :]
            wq[pl.ds(at, 128), :] = (wq[pl.ds(at, 128), :].astype(F32) * scale).astype(BF16)
            return carry

        lax.fori_loop(0, 16, query_block, 0)
        sums[...] = jnp.zeros_like(sums)

    def step_do(_):
        rows = lax.broadcasted_iota(jnp.int32, (32, FEAT), 0)
        cols = lax.broadcasted_iota(jnp.int32, (32, FEAT), 1)
        spread = jnp.where(rows == cols // 64, 1.0, 0.0).astype(BF16)
        copies["oe"].wait()
        powers = jnp.exp2(oe[...].astype(F32)).astype(BF16)
        scale_o[...] = jnp.dot(powers, spread, preferred_element_type=F32) * (1.0 / 128.0)
        copies["oc"].wait()

        def output_block(k, carry):
            at = pl.multiple_of(k * 128, 128)
            scale = scale_o[pl.ds(k, 1), :]
            wo[pl.ds(at, 128), :] = (wo[pl.ds(at, 128), :].astype(F32) * scale).astype(BF16)
            return carry

        lax.fori_loop(0, 8, output_block, 0)

    def step_hg(c):
        came("a_s", c, g.at[c, :, ocore])
        weight = jnp.concatenate([gain[k:k + 1, :] for k in range(FEAT // 128)], axis=1).astype(F32)

        def scaled(p, carry):
            block = g[c, p // 8, (p // 4) % 2, p % 4].astype(F32)
            at = pl.multiple_of(p * 16, 16)
            x[c, pl.ds(at, 16), :] = (block * weight).astype(BF16)
            total = block[:, :128] * block[:, :128]
            for k in range(1, FEAT // 128):
                piece = block[:, k * 128:(k + 1) * 128]
                total = total + piece * piece
            squares[pl.ds(at, 16), :] = total
            return carry

        lax.fori_loop(0, 16, scaled, 0)
        sums[c // 3, c % 3:c % 3 + 1, :] = jnp.sum(squares[...].T, axis=0, keepdims=True)
        part = jnp.dot(x[c], wk[...], preferred_element_type=F32)
        kvp[c] = part.astype(BF16).reshape(2, 4, 2, 16, 128)
        for i, to in enumerate(dev_peers):
            a, b = peers[i]
            send("kvp", c, kvp.at[c, (xlo + a) % 2, (y + b) % 4], kv_in.at[c, i], to, "kvp")
            if c >= 2:
                send("sums", c - 2, sums.at[c - 2], sums_in.at[c - 2, i], to, "sums")

    def step_mm(k):
        c, u = k // 10, k % 10

        part = jnp.dot(x[c], wq[:, u * QH:(u + 1) * QH], preferred_element_type=F32)
        qp[c, u] = part.astype(BF16).reshape(2, 4, 32, QH)
        scatter_b[0](k)

    def keep_queries(c, u, total):
        qown[c, :, u * QH:(u + 1) * QH] = total

    scatter_b = scatter(
        "b", SUM_B, qp, b2, bu, b3, bx, QH, xlo, y, lambda h, w: (h * 4 + w, gy, gz), keep_queries,
    )

    def rows_of(table, c):
        return jnp.concatenate([table[c * 16:c * 16 + 16], table[64 + c * 16:64 + c * 16 + 16]], axis=0)

    def rotated(field, cosine, sine):
        return field * cosine + pltpu.roll(field, 64, 1) * sine

    def step_kx(part):
        came("sums", part, sums_in.at[part])
        total = sums[part]
        for i in range(len(peers)):
            total = total + sums_in[part, i]
        inverse = lax.rsqrt(total * (1.0 / D) + EPS)
        lane = lax.broadcasted_iota(jnp.int32, (32, 256), 1)
        row = lax.broadcasted_iota(jnp.int32, (32, 256), 0)
        chunks = range(3) if part == 0 else range(3, NC)
        for c in chunks:
            spread = jnp.where(lane == row + 32 * gx, inverse[c % 3:c % 3 + 1, :], 0.0)
            factors[c] = jnp.broadcast_to(jnp.sum(spread, axis=1, keepdims=True), (32, 128))
            came("kvp", c, kv_in.at[c])
            total = kvp[c, xlo, y].astype(F32)
            for i in range(len(peers)):
                total = total + kv_in[c, i].astype(F32)
            kv[0, c] = (total.reshape(32, 128) * factors[c]).astype(BF16).reshape(2, 16, 128)
        some = pl.ds(0, 3) if part == 0 else pl.ds(3, 1)
        for place, to in dev_kv:
            send("kv", part, kv.at[0, some], kv.at[place, some], to, "kv")

    def step_ky(_):
        pltpu.make_async_copy(rope, rope, local.at[3]).wait()
        copies["segs"].wait()
        came("kv", 0, kv.at[pl.ds(1, 5), pl.ds(0, 3)])
        came("kv", 1, kv.at[pl.ds(1, 5), pl.ds(3, 1)])

        def in_order(place):
            blocks = [kv[place, c, half] for half in range(2) for c in range(NC)]
            return jnp.concatenate(blocks, axis=0).astype(F32)

        low = lax.broadcasted_iota(jnp.int32, (128, 128), 1) < 64
        for d in range(3):
            at = (2 - d) * 128
            first = in_order(2 * d + odd)
            second = in_order(2 * d + 1 - odd)
            keys = jnp.where(low, first, pltpu.roll(second, 64, 1))
            kb[at:at + 128, :] = rotated(keys, rope[d, 0], rope[d, 1]).astype(BF16)
            vb[at:at + 128, :] = jnp.where(low, pltpu.roll(first, 64, 1), second).astype(BF16)

    def step_at(c):
        cosine, sine = rows_of(rope[0, 0], c), rows_of(rope[0, 1], c)
        factor = factors[c]
        for h in range(8):
            head = qown[c, :, h * 128:(h + 1) * 128] * factor
            qr[h * 32:(h + 1) * 32, :] = rotated(head, cosine, sine).astype(BF16)
        row = lax.broadcasted_iota(jnp.int32, (32, 128), 0)
        lane = lax.broadcasted_iota(jnp.int32, (32, 128), 1)
        mine = segs[pl.ds(gx, 1), :].astype(F32)
        token = (row // 16) * 64 + c * 16 + row % 16
        query_segments = jnp.sum(jnp.where(lane == token, mine, 0.0), axis=1, keepdims=True)
        key_segments = jnp.concatenate([segs[pl.ds((gx + 8 - d) % 8, 1), :] for d in (2, 1, 0)], axis=1).astype(F32)
        row = lax.broadcasted_iota(jnp.int32, (32, 384), 0)
        place = lax.broadcasted_iota(jnp.int32, (32, 384), 1)
        token = (row // 16) * 64 + c * 16 + row % 16
        allowed = (query_segments == key_segments) & (place <= token + 256) & (place >= 256 - 128 * gx)
        masked = jnp.where(allowed, 0.0, -jnp.inf)
        scores = lax.dot_general(qr[...], kb[...], (((1,), (1,)), ((), ())), preferred_element_type=F32)
        scores = (scores * (1.0 / math.sqrt(HD))).reshape(8, 32, 384) + masked[None]
        weights = jnp.exp(scores - jnp.max(scores, axis=2, keepdims=True))
        weights = (weights / jnp.sum(weights, axis=2, keepdims=True)).astype(BF16).reshape(256, 384)
        heads = jnp.dot(weights, vb[...], preferred_element_type=F32).astype(BF16)
        for h in range(8):
            ag[c, xlo, y, :, :, h * 128:(h + 1) * 128] = heads[h * 32:(h + 1) * 32].reshape(2, 16, 128)

    gather_c = gather(
        "c", GATHER_C, SPLIT_C, lambda c, h, w, some: ag.at[c, h, w, :, :, some], QC,
        xlo, y, lambda h, w: (h * 4 + w, gy, gz), lambda k, block: None,
    )

    def step_mo(k):
        c, u = k // 10, k % 10
        i = c * UNITS + u
        rows = ag[c].reshape(256, QC)

        part = jnp.dot(rows, wo[:, u * OH:(u + 1) * OH], preferred_element_type=F32)
        pp[c, u] = part.astype(BF16).reshape(2, 2, 4, 16, OH)
        send("d_s", i, pp.at[c, u, :, ocore], d_in.at[c, u], dev_s, "d_s")

    def step_d0(k):
        c, u = k // 10, k % 10
        came("d_s", c * UNITS + u, d_in.at[c, u])
        for h in range(2):
            for w in range(4):
                dt[c, u, h, w] = pp[c, u, h, core, w] + d_in[c, u, h, w]
        scatter_d[0](k)

    def keep_out(c, u, total):
        columns = slice(u * OH, (u + 1) * OH)
        out[16 * c:16 * c + 16, columns] = (g[c, xhi, core, z, :, columns].astype(F32) + total).astype(BF16)

    scatter_d = scatter(
        "d", SUM_D, dt, d2, du, d3, dx, OH, xhi, z, lambda h, w: (gx, h * 2 + core, w), keep_out,
    )

    table = {
        "DQ": step_dq, "DO": step_do, "HG": step_hg, "MM": step_mm, "KX": step_kx, "KY": step_ky, "AT": step_at,
        "MO": step_mo, "D0": step_d0,
    }
    table.update({"A%d" % i: step for i, step in enumerate(gather_a)})
    table.update({"C%d" % i: step for i, step in enumerate(gather_c)})
    table.update({"B%d" % i: step for i, step in enumerate(scatter_b) if i})
    table.update({"D%d" % i: step for i, step in enumerate(scatter_d) if i})
    for name, c in ORDER:
        if name == "A0" and c == START:
            copies["hid"].wait()
        table[name](c)
    sources = {
        "a_s": g.at[:, :, 0], "sums": sums_in, "kvp": kv_in, "kv": kv.at[pl.ds(1, 5)], "d_s": d_in,
    }
    for group in ("a0", "a1", "b0", "b1", "c0", "c1", "d0", "d1"):
        sources[group] = x.at[0, pl.ds(0, 224)]
    for group, source in sources.items():
        left(group, source)


def shards(hid, gain, segs, qc, qe, kc, ke, oc, oe):
    rope = jnp.asarray(rope_tables())
    kct = kc.transpose(1, 2, 0).reshape(128, FEAT)
    ket = ke.transpose(1, 2, 0).reshape(2, 16)
    hbm, vmem = pl.BlockSpec(memory_space=pl.ANY), pl.BlockSpec(memory_space=pltpu.VMEM)
    scratch = [
        ((FEAT, QC), BF16), ((FEAT, 128), BF16), ((QC, FEAT), BF16), ((128, FEAT), BF16),
        ((16, QC), F32), ((8, FEAT), F32), ((3, 2, 128, HD), F32),
        ((NC, 2, 2, 4, 16, FEAT), BF16), ((NC, 256, FEAT), BF16), ((256, 128), F32),
        ((2, 8, 256), F32), ((2, 7, 8, 256), F32), ((NC, 32, 128), F32),
        ((NC, UNITS, 2, 4, 32, QH), BF16), ((NC, UNITS, 2, 32, QH), BF16), ((NC, UNITS, 2, 32, QH), BF16),
        ((NC, UNITS, 5, 32, QH), BF16), ((NC, UNITS, 4, 32, QH), BF16), ((NC, 32, QC), F32),
        ((NC, 2, 4, 2, 16, 128), BF16), ((NC, 7, 2, 16, 128), BF16), ((6, NC, 2, 16, 128), BF16),
        ((384, 128), BF16), ((384, 128), BF16), ((256, 128), BF16),
        ((NC, 2, 4, 2, 16, QC), BF16), ((NC, UNITS, 2, 2, 4, 16, OH), BF16), ((NC, UNITS, 2, 4, 16, OH), BF16),
        ((NC, UNITS, 2, 4, 16, OH), BF16), ((NC, UNITS, 2, 16, OH), BF16), ((NC, UNITS, 2, 16, OH), BF16),
        ((NC, UNITS, 5, 16, OH), BF16), ((NC, UNITS, 4, 16, OH), BF16),
    ]
    small = [pltpu.VMEM((16, 128), BF16), pltpu.VMEM((8, 128), jnp.int32), pltpu.VMEM((16, 16), jnp.int32)]
    small += [pltpu.SMEM((2, 16), jnp.int32), pltpu.VMEM((8, 32), jnp.int32)]
    scratch = small + [pltpu.VMEM(shape, dtype) for shape, dtype in scratch]
    dma = pltpu.SemaphoreType.DMA
    scratch += [dma((len(SEND),)), dma((len(RECV),)), dma((10,))]
    return pl.pallas_call(
        layer,
        out_shape=jax.ShapeDtypeStruct((64, FEAT), BF16),
        in_specs=[hbm] * 10,
        out_specs=vmem,
        scratch_shapes=scratch,
        compiler_params=pltpu.CompilerParams(collective_id=0, has_side_effects=True, vmem_limit_bytes=60 * 1024 * 1024),
        name="layer",
    )(hid.reshape(NC, 16, FEAT), gain.reshape(16, 128), segs.reshape(8, 128), qc, qe, kct, ket, oc, oe, rope)


def solution(mesh):
    placed = (
        P(("gy", "gz"), "gx"),
        P("gx"),
        P(),
        P("gx", ("gy", "gz")),
        P("gx", ("gy", "gz")),
        P("gx", None, ("gy", "gz")),
        P("gx", None, ("gy", "gz")),
        P(("gy", "gz"), "gx"),
        P(("gy", "gz"), "gx"),
    )
    return jax.shard_map(shards, mesh=mesh, in_specs=placed, out_specs=P(("gy", "gz"), "gx"), check_vma=False)
```

```python
import math

import jax
import jax.numpy as jnp
import numpy as np
from jax import lax
from jax.experimental import pallas as pl
from jax.experimental.pallas import tpu as pltpu
from jax.sharding import PartitionSpec as P

D = 16384
HD = 128
TOKENS = 1024
THETA = 500000.0
EPS = 1e-05
NC = 4
FEAT = 2048
QC = 1024
QH, OH = 512, 1024
F32, BF16 = jnp.float32, jnp.bfloat16
MESH = pl.DeviceIdType.MESH

UNITS = 2
GATHER_A = "b0b0"
GATHER_C = "bb00"
SPLIT_A = "1111"
SPLIT_C = "1111"
SUM_B = "yyyyxgyy"
SUM_D = "ggyyxyyg"
GATHER_COPIES = ("x", "p", "m", "pc", "mc", "r")


def semaphore_names():
    names = []
    for c in range(NC):
        names += [("a_s", c), ("kvp", c)]
        for letter, modes, split in (("a_", GATHER_A, SPLIT_A), ("c_", GATHER_C, SPLIT_C)):
            for k in range(c * 10, c * 10 + int(split[c])):
                names += [(letter + kind, k) for kind in GATHER_COPIES + (("x2",) if modes[c] == "b" else ())]
        for i in (2 * c, 2 * c + 1):
            names += [("d_s", i)]
            for letter, modes in (("b_", SUM_B), ("d_", SUM_D)):
                names += [(letter + kind, i) for kind in ("2", "3") + (("x",) if modes[i] != "g" else ())]
    return names + [("sums", 0), ("sums", 1), ("kv", 0), ("kv", 1)]


RECV = {name: i for i, name in enumerate(semaphore_names())}
SEND = ["a0", "a1", "a_s", "b0", "b1", "sums", "kvp", "kv", "c0", "c1", "d_s", "d0", "d1"]
SEND = {name: i for i, name in enumerate(SEND)}

ORDER = (
    ("A0", 0), ("A0", 10), ("DQ", 0), ("A0", 20), ("A1", 0), ("A1", 10), ("A0", 30), ("A2", 0), ("DO", 0), ("A1", 30),
    ("A2", 10), ("A3", 0), ("A1", 20), ("HG", 0), ("MM", 1), ("A3", 10), ("A2", 30), ("A2", 20), ("MM", 0),
    ("HG", 1), ("B2", 1), ("MM", 10), ("A3", 30), ("B2", 0), ("A3", 20), ("MM", 11), ("HG", 2), ("B2", 10),
    ("HG", 3), ("MM", 20), ("B2", 11), ("MM", 31), ("B3", 1), ("KX", 0), ("B3", 10), ("KX", 1), ("B3", 11),
    ("MM", 21), ("B1", 20), ("B3", 0), ("MM", 30), ("B2", 31), ("B4", 1), ("KY", 0), ("B2", 21), ("B4", 10),
    ("B4", 11), ("AT", 1), ("C0", 10), ("B2", 20), ("B4", 0), ("AT", 0), ("B2", 30), ("C0", 0),
    ("B3", 31), ("C1", 10), ("B4", 20), ("B4", 21), ("B3", 30), ("AT", 2), ("C0", 20), ("C2", 10), ("C1", 0),
    ("B4", 31), ("B4", 30), ("AT", 3), ("C0", 30), ("C1", 20), ("C2", 0), ("C3", 10), ("MO", 11), ("C1", 30),
    ("MO", 10), ("D0", 11), ("C2", 20), ("C3", 0), ("MO", 1), ("D0", 10), ("MO", 0), ("D0", 1), ("C2", 30),
    ("D2", 11), ("C3", 20), ("D0", 0), ("MO", 20), ("MO", 21), ("D2", 1), ("D2", 10), ("D0", 20), ("C3", 30),
    ("MO", 30), ("D0", 21), ("MO", 31), ("D3", 11), ("D0", 30), ("D3", 10), ("D0", 31), ("D2", 30), ("D2", 21),
    ("D4", 1), ("D1", 20), ("D4", 11), ("D2", 0), ("D2", 31), ("D3", 30), ("D3", 21), ("D2", 20), ("D4", 10),
    ("D4", 30), ("D4", 20), ("D4", 0), ("D4", 21), ("D4", 31),
)


START = [c for name, c in ORDER if name == "A0"][0]


def rope_tables():
    frequency = np.exp(np.arange(HD // 2, dtype=np.float64) * (-2.0 * math.log(THETA) / HD))
    angles = np.arange(TOKENS, dtype=np.float64)[:, None] * frequency[None, :]
    cosine, sine = np.cos(angles), np.sin(angles)
    cosine = np.concatenate([cosine, cosine], axis=1).astype(np.float32)
    sine = np.concatenate([-sine, sine], axis=1).astype(np.float32)
    return np.stack([cosine.reshape(8, 128, HD), sine.reshape(8, 128, HD)], axis=1)


def layer(
    hid, gain_hbm, segs_hbm, qc, qe_hbm, kc, ke_hbm, oc, oe_hbm, rope_hbm, out,
    gain, segs, qe, ke, oe, result,
    wq, wk, wo, kct, scale_q, scale_o, rope,
    g, x, squares, sums, sums_in, factors,
    qp, b2, bu, b3, bx, qown,
    kvp, kv_in, kv, kb, vb, qr,
    ag, pp, d_in, dt, d2, du, d3, dx,
    send_sem, recv_sem, local,
):
    gx, gy, gz = lax.axis_index("gx"), lax.axis_index("gy"), lax.axis_index("gz")
    xlo, y, xhi, core, z = gx // 4, gx % 4, gy // 2, gy % 2, gz
    yp, ym, y2 = (y + 1) % 4, (y + 3) % 4, (y + 2) % 4
    zp, zm, z2 = (z + 1) % 4, (z + 3) % 4, (z + 2) % 4
    oxlo, oxhi, ocore = 1 - xlo, 1 - xhi, 1 - core
    odd = z % 2
    zo = z + 1 - 2 * odd
    dev_s = (gx, xhi * 2 + ocore, gz)
    dev_xhi = (gx, oxhi * 2 + core, gz)
    dev_zp, dev_zm = (gx, gy, zp), (gx, gy, zm)
    dev_xlo = (oxlo * 4 + y, gy, gz)
    dev_yp, dev_ym = (xlo * 4 + yp, gy, gz), (xlo * 4 + ym, gy, gz)
    peers = [(a, b) for a in range(2) for b in range(4) if (a, b) != (0, 0)]
    dev_peers = [(((xlo + a) % 2) * 4 + (y + b) % 4, gy, gz) for a, b in peers]
    dev_kv = [(1, (gx, gy, zo))]
    for d in (1, 2):
        dev_kv += [(2 * d, ((gx + d) % 8, gy, z)), (2 * d + 1, ((gx + d) % 8, gy, zo))]

    barrier = pltpu.get_barrier_semaphore()
    greeted = [(gx, oxhi * 2 + core, (z + d) % 4) for d in (1, 3, 0)] + [(gx, gy, (z + d) % 4) for d in (1, 3)]
    greeted += [dev_s] + dev_peers
    greeted += [((gx + d) % 8, gy, zo) for d in (1, 2, 6, 7)]
    for other in greeted:
        pl.semaphore_signal(barrier, inc=1, device_id=other, device_id_type=MESH)

    copies = {}

    def fetch(name, index, src, dst):
        copies[name] = pltpu.make_async_copy(src, dst, local.at[index])
        copies[name].start()

    fetch("hid", 0, hid, g.at[:, xhi, core, z])
    fetch("ke", 5, ke_hbm, ke)
    fetch("qe", 6, qe_hbm, qe)
    fetch("kc", 1, kc, kct)
    fetch("qc", 2, qc, wq)
    for d in range(3):
        pltpu.make_async_copy(rope_hbm.at[(gx + 8 - d) % 8], rope.at[d], local.at[3]).start()
    fetch("gain", 7, gain_hbm, gain)
    fetch("segs", 8, segs_hbm, segs)
    fetch("oe", 9, oe_hbm, oe)
    fetch("oc", 4, oc, wo)

    pl.semaphore_wait(barrier, len(greeted))

    def send(name, i, src, dst, to, group):
        pltpu.make_async_remote_copy(
            src_ref=src, dst_ref=dst, send_sem=send_sem.at[SEND[group]], recv_sem=recv_sem.at[RECV[name, i]],
            device_id=to, device_id_type=MESH,
        ).start()

    def came(name, i, dst):
        pltpu.make_async_remote_copy(
            src_ref=dst, dst_ref=dst, send_sem=send_sem.at[0], recv_sem=recv_sem.at[RECV[name, i]],
            device_id=dev_s, device_id_type=MESH,
        ).wait_recv()

    def left(group, src):
        pltpu.make_async_remote_copy(
            src_ref=src, dst_ref=src, send_sem=send_sem.at[SEND[group]], recv_sem=recv_sem.at[0],
            device_id=dev_s, device_id_type=MESH,
        ).wait_send()

    def gather(letter, modes, split, blocks, width, h, w, device, neighbour):
        oh, wp, wm, w2 = 1 - h, (w + 1) % 4, (w + 3) % 4, (w + 2) % 4
        across, plus, minus = device(oh, w), device(h, wp), device(h, wm)

        def mode(k):
            return modes[k // 10]

        def buffer(k, column, at, piece=0, pieces=1):
            count = int(split[k // 10]) * pieces
            return blocks(k // 10, column, at, pl.ds((k % 10 * pieces + piece) * (width // count), width // count))

        def copy(kind, k, block, to):
            send(letter + "_" + kind, k, block, block, to, letter + str(k // 20))

        def await_block(kind, k, block):
            came(letter + "_" + kind, k, block)

        def first(k):
            own = buffer(k, h, w)
            copy("x", k, own, across)
            copy("p", k, own, plus)
            copy("m", k, own, minus)
            neighbour(k, own)
            if mode(k) == "D":
                copy("r", k, own, device(h, w2))
                copy("pc", k, own, device(oh, wp))
                copy("mc", k, own, device(oh, wm))
                copy("r", k, own, device(oh, w2))

        def second(k):
            if mode(k) == "b":
                await_block("p", k, buffer(k, h, wm))
                copy("r", k, buffer(k, h, wm, 0, 2), plus)
                neighbour(k, buffer(k, h, wm))
                await_block("m", k, buffer(k, h, wp))
                copy("r", k, buffer(k, h, wp, 1, 2), minus)
                neighbour(k, buffer(k, h, wp))
            block = buffer(k, oh, w)
            await_block("x", k, block)
            copy("pc", k, block, plus)
            copy("mc", k, block, minus)
            neighbour(k, block)

        def third(k):
            if mode(k) == "b":
                block = buffer(k, h, w2)
                await_block("r", k, block)
                copy("x2", k, block, across)
                neighbour(k, block)
                return
            await_block("p", k, buffer(k, h, wm))
            await_block("pc", k, buffer(k, oh, wm))
            copy("r", k, buffer(k, 0, wm), plus)
            await_block("m", k, buffer(k, h, wp))
            await_block("mc", k, buffer(k, oh, wp))
            copy("r", k, buffer(k, 1, wp), minus)
            neighbour(k, buffer(k, slice(None), wm))
            neighbour(k, buffer(k, slice(None), wp))

        def fourth(k):
            if mode(k) == "b":
                for kind, at in (("pc", wm), ("mc", wp), ("x2", w2)):
                    block = buffer(k, oh, at)
                    await_block(kind, k, block)
                    neighbour(k, block)
                return
            if mode(k) == "D":
                await_block("x", k, buffer(k, oh, w))
                neighbour(k, buffer(k, oh, w))
                for kind, at in (("p", wm), ("m", wp)):
                    await_block(kind, k, buffer(k, h, at))
                    await_block(kind + "c", k, buffer(k, oh, at))
                    neighbour(k, buffer(k, slice(None), at))
            both = buffer(k, slice(None), w2)
            await_block("r", k, both)
            neighbour(k, both)

        return first, second, third, fourth

    def scatter(letter, modes, part, r2, ru, r3, rx, width, h, w, device, finish):
        oh, wp, wm, w2 = 1 - h, (w + 1) % 4, (w + 3) % 4, (w + 2) % 4
        across, plus, minus = device(oh, w), device(h, wp), device(h, wm)
        low, high = pl.ds(0, width // 2), pl.ds(width // 2, width // 2)

        def copy(kind, k, src, dst, to):
            i = k // 10 * UNITS + k % 10
            send(letter + "_" + kind, i, src, dst, to, letter + str(k // 20))

        def await_blocks(kind, k, blocks):
            came(letter + "_" + kind, k // 10 * UNITS + k % 10, blocks)

        def mode(k):
            return modes[k // 10 * UNITS + k % 10]

        def begin(k):
            c, u = k // 10, k % 10
            if mode(k) == "x":
                copy("x", k, part.at[c, u, oh], rx.at[c, u], across)
                return
            copy("2", k, part.at[c, u, 0, w2], r2.at[c, u, 0], plus)
            copy("2", k, part.at[c, u, 1, w2], r2.at[c, u, 1], minus)
            if mode(k) == "g":
                copy("3", k, part.at[c, u, 1, wp], r3.at[c, u, 2 - h], device(1, wp))
                copy("3", k, part.at[c, u, 0, wm], r3.at[c, u, 3 + h], device(0, wm))
                copy("3", k, part.at[c, u, oh, w], r3.at[c, u, 0], across)
            else:
                copy("3", k, part.at[c, u, 1, wp], r3.at[c, u, 2], plus)
                copy("3", k, part.at[c, u, 0, wm], r3.at[c, u, 3], minus)

        def one(k):
            c, u = k // 10, k % 10
            await_blocks("x", k, rx.at[c, u])

            def add(at):
                part[c, u, h, at] = part[c, u, h, at] + rx[c, u, at]

            add(w2)
            copy("2", k, part.at[c, u, h, w2, :, low], r2.at[c, u, 0, :, low], plus)
            copy("2", k, part.at[c, u, h, w2, :, high], r2.at[c, u, 1, :, high], minus)
            add(wp)
            copy("3", k, part.at[c, u, h, wp, :, high], r3.at[c, u, 1, :, high], plus)
            add(wm)
            copy("3", k, part.at[c, u, h, wm, :, low], r3.at[c, u, 3, :, low], minus)
            add(w)

        def two(k):
            c, u = k // 10, k % 10
            if mode(k) == "x":
                await_blocks("2", k, r2.at[c, u, 0])
                ru[c, u, 0, :, low] = part[c, u, h, wp, :, low] + r2[c, u, 0, :, low]
                copy("3", k, ru.at[c, u, 0, :, low], r3.at[c, u, 1, :, low], plus)
                ru[c, u, 1, :, high] = part[c, u, h, wm, :, high] + r2[c, u, 1, :, high]
                copy("3", k, ru.at[c, u, 1, :, high], r3.at[c, u, 3, :, high], minus)
                return
            await_blocks("2", k, r2.at[c, u])
            ru[c, u, 0] = part[c, u, 0, wp] + r2[c, u, 0]
            if mode(k) == "g":
                copy("3", k, ru.at[c, u, 0], r3.at[c, u, 1 + h], device(0, wp))
            else:
                copy("3", k, ru.at[c, u, 0], r3.at[c, u, 1], plus)
            ru[c, u, 1] = part[c, u, 1, wm] + r2[c, u, 1]
            if mode(k) == "g":
                copy("3", k, ru.at[c, u, 1], r3.at[c, u, 4 - h], device(1, wm))
            else:
                copy("3", k, ru.at[c, u, 1], r3.at[c, u, 4], minus)

        def three(k):
            c, u = k // 10, k % 10
            await_blocks("3", k, r3.at[c, u, pl.ds(1, 4)])
            total = part[c, u, oh, w].astype(F32) + r3[c, u, 1 + oh].astype(F32) + r3[c, u, 3 + oh].astype(F32)
            part[c, u, oh, w] = total.astype(BF16)
            copy("x", k, part.at[c, u, oh, w], r3.at[c, u, 0], across)

        def four(k):
            c, u = k // 10, k % 10
            total = part[c, u, h, w].astype(F32)
            if mode(k) == "g":
                await_blocks("3", k, r3.at[c, u])
                slots = range(5)
            elif mode(k) == "y":
                await_blocks("x", k, r3.at[c, u, 0])
                slots = (0, 1 + h, 3 + h)
            else:
                await_blocks("3", k, r3.at[c, u, pl.ds(1, 2)])
                slots = (1, 3)
            for slot in slots:
                total = total + r3[c, u, slot].astype(F32)
            finish(c, u, total)

        return begin, one, two, three, four

    def to_core(k, block):
        send("a_s", k // 10, block, block, dev_s, "a_s")

    gather_a = gather(
        "a", GATHER_A, SPLIT_A, lambda c, h, w, some: g.at[c, h, core, w, :, some], FEAT,
        xhi, z, lambda h, w: (gx, h * 2 + core, w), to_core,
    )

    def step_dq(_):
        rows = lax.broadcasted_iota(jnp.int32, (16, QC), 0)
        cols = lax.broadcasted_iota(jnp.int32, (16, QC), 1)
        spread = jnp.where(rows == cols // 64, 1.0, 0.0).astype(BF16)
        copies["qe"].wait()
        copies["ke"].wait()
        copies["gain"].wait()
        powers = jnp.exp2(qe[...].astype(F32)).astype(BF16)
        scale_q[...] = jnp.dot(powers, spread, preferred_element_type=F32) * (1.0 / 128.0)
        copies["kc"].wait()
        lane = lax.broadcasted_iota(jnp.int32, (1, 128), 1)

        def key_block(k, carry):
            at = pl.multiple_of(k * 128, 128)
            e = jnp.where(lane < 64, ke[0, k], ke[1, k]).astype(F32)
            scale = jnp.exp2(e) * (1.0 / 128.0)
            block = kct[:, pl.ds(at, 128)].astype(F32).T
            wk[pl.ds(at, 128), :] = (block * scale).astype(BF16)
            return carry

        lax.fori_loop(0, 16, key_block, 0)
        copies["qc"].wait()

        def query_block(k, carry):
            at = pl.multiple_of(k * 128, 128)
            scale = scale_q[pl.ds(k, 1), :]
            wq[pl.ds(at, 128), :] = (wq[pl.ds(at, 128), :].astype(F32) * scale).astype(BF16)
            return carry

        lax.fori_loop(0, 16, query_block, 0)
        sums[...] = jnp.zeros_like(sums)

    def step_do(_):
        rows = lax.broadcasted_iota(jnp.int32, (32, FEAT), 0)
        cols = lax.broadcasted_iota(jnp.int32, (32, FEAT), 1)
        spread = jnp.where(rows == cols // 64, 1.0, 0.0).astype(BF16)
        copies["oe"].wait()
        powers = jnp.exp2(oe[...].astype(F32)).astype(BF16)
        scale_o[...] = jnp.dot(powers, spread, preferred_element_type=F32) * (1.0 / 128.0)
        copies["oc"].wait()

        def output_block(k, carry):
            at = pl.multiple_of(k * 128, 128)
            scale = scale_o[pl.ds(k, 1), :]
            wo[pl.ds(at, 128), :] = (wo[pl.ds(at, 128), :].astype(F32) * scale).astype(BF16)
            return carry

        lax.fori_loop(0, 8, output_block, 0)

    def step_hg(c):
        came("a_s", c, g.at[c, :, ocore])
        weight = jnp.concatenate([gain[k:k + 1, :] for k in range(FEAT // 128)], axis=1).astype(F32)

        def scaled(p, carry):
            block = g[c, p // 8, (p // 4) % 2, p % 4].astype(F32)
            at = pl.multiple_of(p * 16, 16)
            x[c, pl.ds(at, 16), :] = (block * weight).astype(BF16)
            total = block[:, :128] * block[:, :128]
            for k in range(1, FEAT // 128):
                piece = block[:, k * 128:(k + 1) * 128]
                total = total + piece * piece
            squares[pl.ds(at, 16), :] = total
            return carry

        lax.fori_loop(0, 16, scaled, 0)
        sums[c // 3, c % 3:c % 3 + 1, :] = jnp.sum(squares[...].T, axis=0, keepdims=True)
        part = jnp.dot(x[c], wk[...], preferred_element_type=F32)
        kvp[c] = part.astype(BF16).reshape(2, 4, 2, 16, 128)
        for i, to in enumerate(dev_peers):
            a, b = peers[i]
            send("kvp", c, kvp.at[c, (xlo + a) % 2, (y + b) % 4], kv_in.at[c, i], to, "kvp")
            if c >= 2:
                send("sums", c - 2, sums.at[c - 2], sums_in.at[c - 2, i], to, "sums")

    def step_mm(k):
        c, u = k // 10, k % 10

        part = jnp.dot(x[c], wq[:, u * QH:(u + 1) * QH], preferred_element_type=F32)
        qp[c, u] = part.astype(BF16).reshape(2, 4, 32, QH)
        scatter_b[0](k)

    def keep_queries(c, u, total):
        qown[c, :, u * QH:(u + 1) * QH] = total

    scatter_b = scatter(
        "b", SUM_B, qp, b2, bu, b3, bx, QH, xlo, y, lambda h, w: (h * 4 + w, gy, gz), keep_queries,
    )

    def rows_of(table, c):
        return jnp.concatenate([table[c * 16:c * 16 + 16], table[64 + c * 16:64 + c * 16 + 16]], axis=0)

    def rotated(field, cosine, sine):
        return field * cosine + pltpu.roll(field, 64, 1) * sine

    def step_kx(part):
        came("sums", part, sums_in.at[part])
        total = sums[part]
        for i in range(len(peers)):
            total = total + sums_in[part, i]
        inverse = lax.rsqrt(total * (1.0 / D) + EPS)
        lane = lax.broadcasted_iota(jnp.int32, (32, 256), 1)
        row = lax.broadcasted_iota(jnp.int32, (32, 256), 0)
        chunks = range(3) if part == 0 else range(3, NC)
        for c in chunks:
            spread = jnp.where(lane == row + 32 * gx, inverse[c % 3:c % 3 + 1, :], 0.0)
            factors[c] = jnp.broadcast_to(jnp.sum(spread, axis=1, keepdims=True), (32, 128))
            came("kvp", c, kv_in.at[c])
            total = kvp[c, xlo, y].astype(F32)
            for i in range(len(peers)):
                total = total + kv_in[c, i].astype(F32)
            kv[0, c] = (total.reshape(32, 128) * factors[c]).astype(BF16).reshape(2, 16, 128)
        some = pl.ds(0, 3) if part == 0 else pl.ds(3, 1)
        for place, to in dev_kv:
            send("kv", part, kv.at[0, some], kv.at[place, some], to, "kv")

    def step_ky(_):
        pltpu.make_async_copy(rope, rope, local.at[3]).wait()
        copies["segs"].wait()
        came("kv", 0, kv.at[pl.ds(1, 5), pl.ds(0, 3)])
        came("kv", 1, kv.at[pl.ds(1, 5), pl.ds(3, 1)])

        def in_order(place):
            blocks = [kv[place, c, half] for half in range(2) for c in range(NC)]
            return jnp.concatenate(blocks, axis=0).astype(F32)

        low = lax.broadcasted_iota(jnp.int32, (128, 128), 1) < 64
        for d in range(3):
            at = (2 - d) * 128
            first = in_order(2 * d + odd)
            second = in_order(2 * d + 1 - odd)
            keys = jnp.where(low, first, pltpu.roll(second, 64, 1))
            kb[at:at + 128, :] = rotated(keys, rope[d, 0], rope[d, 1]).astype(BF16)
            vb[at:at + 128, :] = jnp.where(low, pltpu.roll(first, 64, 1), second).astype(BF16)

    def step_at(c):
        cosine, sine = rows_of(rope[0, 0], c), rows_of(rope[0, 1], c)
        factor = factors[c]
        for h in range(8):
            head = qown[c, :, h * 128:(h + 1) * 128] * factor
            qr[h * 32:(h + 1) * 32, :] = rotated(head, cosine, sine).astype(BF16)
        row = lax.broadcasted_iota(jnp.int32, (32, 128), 0)
        lane = lax.broadcasted_iota(jnp.int32, (32, 128), 1)
        mine = segs[pl.ds(gx, 1), :].astype(F32)
        token = (row // 16) * 64 + c * 16 + row % 16
        query_segments = jnp.sum(jnp.where(lane == token, mine, 0.0), axis=1, keepdims=True)
        key_segments = jnp.concatenate([segs[pl.ds((gx + 8 - d) % 8, 1), :] for d in (2, 1, 0)], axis=1).astype(F32)
        row = lax.broadcasted_iota(jnp.int32, (32, 384), 0)
        place = lax.broadcasted_iota(jnp.int32, (32, 384), 1)
        token = (row // 16) * 64 + c * 16 + row % 16
        allowed = (query_segments == key_segments) & (place <= token + 256) & (place >= 256 - 128 * gx)
        masked = jnp.where(allowed, 0.0, -jnp.inf)
        scores = lax.dot_general(qr[...], kb[...], (((1,), (1,)), ((), ())), preferred_element_type=F32)
        scores = (scores * (1.0 / math.sqrt(HD))).reshape(8, 32, 384) + masked[None]
        weights = jnp.exp(scores - jnp.max(scores, axis=2, keepdims=True))
        weights = (weights / jnp.sum(weights, axis=2, keepdims=True)).astype(BF16).reshape(256, 384)
        heads = jnp.dot(weights, vb[...], preferred_element_type=F32).astype(BF16)
        for h in range(8):
            ag[c, xlo, y, :, :, h * 128:(h + 1) * 128] = heads[h * 32:(h + 1) * 32].reshape(2, 16, 128)

    gather_c = gather(
        "c", GATHER_C, SPLIT_C, lambda c, h, w, some: ag.at[c, h, w, :, :, some], QC,
        xlo, y, lambda h, w: (h * 4 + w, gy, gz), lambda k, block: None,
    )

    def step_mo(k):
        c, u = k // 10, k % 10
        i = c * UNITS + u
        rows = ag[c].reshape(256, QC)

        part = jnp.dot(rows, wo[:, u * OH:(u + 1) * OH], preferred_element_type=F32)
        pp[c, u] = part.astype(BF16).reshape(2, 2, 4, 16, OH)
        send("d_s", i, pp.at[c, u, :, ocore], d_in.at[c, u], dev_s, "d_s")

    def step_d0(k):
        c, u = k // 10, k % 10
        came("d_s", c * UNITS + u, d_in.at[c, u])
        for h in range(2):
            for w in range(4):
                dt[c, u, h, w] = pp[c, u, h, core, w] + d_in[c, u, h, w]
        scatter_d[0](k)

    def keep_out(c, u, total):
        columns = slice(u * OH, (u + 1) * OH)
        result[16 * c:16 * c + 16, columns] = (g[c, xhi, core, z, :, columns].astype(F32) + total).astype(BF16)
        block = (pl.ds(16 * c, 16), pl.ds(u * OH, OH))
        fetch("out%d" % (c * UNITS + u), 10 + c * UNITS + u, result.at[block], out.at[block])

    scatter_d = scatter(
        "d", SUM_D, dt, d2, du, d3, dx, OH, xhi, z, lambda h, w: (gx, h * 2 + core, w), keep_out,
    )

    table = {
        "DQ": step_dq, "DO": step_do, "HG": step_hg, "MM": step_mm, "KX": step_kx, "KY": step_ky, "AT": step_at,
        "MO": step_mo, "D0": step_d0,
    }
    table.update({"A%d" % i: step for i, step in enumerate(gather_a)})
    table.update({"C%d" % i: step for i, step in enumerate(gather_c)})
    table.update({"B%d" % i: step for i, step in enumerate(scatter_b) if i})
    table.update({"D%d" % i: step for i, step in enumerate(scatter_d) if i})
    for name, c in ORDER:
        if name == "A0" and c == START:
            copies["hid"].wait()
        table[name](c)
    for i in range(NC * UNITS):
        copies["out%d" % i].wait()
    sources = {
        "a_s": g.at[:, :, 0], "sums": sums_in, "kvp": kv_in, "kv": kv.at[pl.ds(1, 5)], "d_s": d_in,
    }
    for group in ("a0", "a1", "b0", "b1", "c0", "c1", "d0", "d1"):
        sources[group] = x.at[0, pl.ds(0, 224)]
    for group, source in sources.items():
        left(group, source)


def shards(hid, gain, segs, qc, qe, kc, ke, oc, oe):
    rope = jnp.asarray(rope_tables())
    kct = kc.transpose(1, 2, 0).reshape(128, FEAT)
    ket = ke.transpose(1, 2, 0).reshape(2, 16)
    hbm = pl.BlockSpec(memory_space=pl.ANY)
    scratch = [
        ((FEAT, QC), BF16), ((FEAT, 128), BF16), ((QC, FEAT), BF16), ((128, FEAT), BF16),
        ((16, QC), F32), ((8, FEAT), F32), ((3, 2, 128, HD), F32),
        ((NC, 2, 2, 4, 16, FEAT), BF16), ((NC, 256, FEAT), BF16), ((256, 128), F32),
        ((2, 8, 256), F32), ((2, 7, 8, 256), F32), ((NC, 32, 128), F32),
        ((NC, UNITS, 2, 4, 32, QH), BF16), ((NC, UNITS, 2, 32, QH), BF16), ((NC, UNITS, 2, 32, QH), BF16),
        ((NC, UNITS, 5, 32, QH), BF16), ((NC, UNITS, 4, 32, QH), BF16), ((NC, 32, QC), F32),
        ((NC, 2, 4, 2, 16, 128), BF16), ((NC, 7, 2, 16, 128), BF16), ((6, NC, 2, 16, 128), BF16),
        ((384, 128), BF16), ((384, 128), BF16), ((256, 128), BF16),
        ((NC, 2, 4, 2, 16, QC), BF16), ((NC, UNITS, 2, 2, 4, 16, OH), BF16), ((NC, UNITS, 2, 4, 16, OH), BF16),
        ((NC, UNITS, 2, 4, 16, OH), BF16), ((NC, UNITS, 2, 16, OH), BF16), ((NC, UNITS, 2, 16, OH), BF16),
        ((NC, UNITS, 5, 16, OH), BF16), ((NC, UNITS, 4, 16, OH), BF16),
    ]
    small = [pltpu.VMEM((16, 128), BF16), pltpu.VMEM((8, 128), jnp.int32), pltpu.VMEM((16, 16), jnp.int32)]
    small += [pltpu.SMEM((2, 16), jnp.int32), pltpu.VMEM((8, 32), jnp.int32), pltpu.VMEM((64, FEAT), BF16)]
    scratch = small + [pltpu.VMEM(shape, dtype) for shape, dtype in scratch]
    dma = pltpu.SemaphoreType.DMA
    scratch += [dma((len(SEND),)), dma((len(RECV),)), dma((10 + NC * UNITS,))]
    return pl.pallas_call(
        layer,
        out_shape=jax.ShapeDtypeStruct((64, FEAT), BF16),
        in_specs=[hbm] * 10,
        out_specs=hbm,
        scratch_shapes=scratch,
        compiler_params=pltpu.CompilerParams(collective_id=0, has_side_effects=True, vmem_limit_bytes=60 * 1024 * 1024),
        name="layer",
    )(hid.reshape(NC, 16, FEAT), gain.reshape(16, 128), segs.reshape(8, 128), qc, qe, kct, ket, oc, oe, rope)


def solution(mesh):
    placed = (
        P(("gy", "gz"), "gx"),
        P("gx"),
        P(),
        P("gx", ("gy", "gz")),
        P("gx", ("gy", "gz")),
        P("gx", None, ("gy", "gz")),
        P("gx", None, ("gy", "gz")),
        P(("gy", "gz"), "gx"),
        P(("gy", "gz"), "gx"),
    )
    return jax.shard_map(shards, mesh=mesh, in_specs=placed, out_specs=P(("gy", "gz"), "gx"), check_vma=False)
```
